512 devices in a mesh: ctx: 32 (over y, x), head: 16 (over z, core).
Axes of the slice: x: 4, y: 8, z: 8, core: 2. Of those that a mesh axis runs over, the one named last changes fastest.
Arguments:
- queries: bfloat16 [16384, 8192], P('ctx', 'head'), may hold values from -2 to 2
- keys: bfloat16 [16384, 8192], P('ctx', 'head'), may hold values from -2 to 2
- values: bfloat16 [16384, 8192], P('ctx', 'head'), may hold values from -6 to 6
- out_grad: bfloat16 [16384, 8192], P('ctx', 'head'), may hold values from -6 to 6
- decay_rate: float32 [64], P('head'), may hold values from 3.0517578e-06 to 0.034, as said below
- gain: float32 [8192], P('head'), may hold values from 0.1 to 1.9
Outputs:
- normed: bfloat16 [16384, 8192], P('ctx', 'head')
- query_gradient: bfloat16 [16384, 8192], P('ctx', 'head')
- key_gradient: bfloat16 [16384, 8192], P('ctx', 'head')
- value_gradient: bfloat16 [16384, 8192], P('ctx', 'head')
The draws below stay inside these ranges and needn't reach their ends.
Inputs may be any that keep to these rules, and one draw needn't show every extreme that they name: `decay_rate`: rates are positive.
All inputs are finite; a program needn't handle non-finite values.
Results may differ from the reference program's by a relative error of at most 0.0051.
Values sent between devices are 32-bit elements; how exact they have to be, the bound alone decides.
No kernel may reach another device: no remote copies, remote signals or barrier semaphores. Data moves between devices by JAX's collectives and lax.ppermute only.
A program may use at most 64 MiB of HBM per device.

```python
import math
import jax
import jax.numpy as jnp
from jax import lax

DH = 128
TOK_DEV = 512
HEADS = 64
TOKENS = 16384
N_CTX = 32


def draw_decay_rate(key, part):
    key = jax.random.fold_in(key, 11)
    first, second, third = jax.random.split(key, 3)
    share = 0.5
    quick = jax.random.uniform(first, (HEADS,)) < share
    quick_rate = jnp.exp(jax.random.uniform(second, (HEADS,), minval=math.log(1.0 / 50.0), maxval=math.log(1.0 / 30.0)))
    slow_rate = jnp.exp(jax.random.uniform(third, (HEADS,), minval=math.log(0.05), maxval=math.log(2.0))) / TOKENS
    return jnp.where(quick, quick_rate, slow_rate).astype(jnp.float32)


def level_of(stream_key, dims, shards, smallest, largest):
    factor_of, own = 1.0, jax.random.fold_in(stream_key, 6)
    for position, shards_of in shards:
        steps = jnp.exp(jax.random.uniform(jax.random.fold_in(own, position), (shards_of,), jnp.float32, smallest / len(shards), largest / len(shards)))
        factor_of = factor_of * jnp.repeat(steps, dims[position] // shards_of).reshape([-1 if axis == position else 1 for axis in range(len(dims))])
    return factor_of


def noise(key, shape, deviation, reach, cuts=(), kind=jnp.bfloat16):
    level = level_of(key, shape, cuts, -0.22, 0.18) if cuts else 1.0
    entries = jax.random.normal(key, shape, jnp.float32) * deviation * level
    return jnp.minimum(jnp.maximum(entries, -reach), reach).astype(kind)


def setup_inputs(seed: int = 0) -> dict:
    key_list = jax.random.split(jax.random.key(seed), 7)
    queries = noise(key_list[0], (TOKENS, HEADS * DH), 0.3, 2.0, ((0, 32), (1, 16)))
    keys = noise(key_list[1], (TOKENS, HEADS * DH), 0.3, 2.0, ((0, 32), (1, 16)))
    values = noise(key_list[2], (TOKENS, HEADS * DH), 1.0, 6.0, ((0, 32), (1, 16)))
    out_grad = noise(key_list[3], (TOKENS, HEADS * DH), 1.0, 6.0, ((0, 32), (1, 16)))
    decay_rate = draw_decay_rate(jax.random.fold_in(key_list[6], 71), 0)
    gain = jnp.clip(1.0 + 0.18 * jax.random.normal(key_list[5], (HEADS * DH,), jnp.float32), 0.1, 1.9)
    return {"queries": queries, "keys": keys, "values": values, "out_grad": out_grad, "decay_rate": decay_rate, "gain": gain}


def decay_table(rate, count):
    pos = jnp.arange(count, dtype=jnp.float32)
    diff = pos[:, None] - pos[None, :]
    return jnp.where(diff[None] >= 0, jnp.exp(-rate[:, None, None] * jnp.maximum(diff, 0.0)[None]), 0.0)

def reference(queries, keys, values, out_grad, decay_rate, gain):
    highest_precision = lax.Precision.HIGHEST
    single_float = jnp.float32
    shape4 = (N_CTX, TOK_DEV, HEADS, DH)
    qall = queries.reshape(shape4)
    kall = keys.reshape(shape4)
    vall = values.reshape(shape4)
    pos = jnp.arange(TOK_DEV, dtype=single_float)
    table = decay_table(decay_rate, TOK_DEV)
    start_weight = jnp.exp(-decay_rate[None, :] * (pos[:, None] + 1.0))[..., None]
    end_weight = jnp.exp(-decay_rate[None, :] * (TOK_DEV - 1.0 - pos[:, None]))[..., None]
    tail_weight = jnp.exp(-decay_rate[None, :] * (TOK_DEV - pos[:, None]))[..., None]
    head_weight = jnp.exp(-decay_rate[None, :] * pos[:, None])[..., None]
    block_decay = jnp.exp(-decay_rate * TOK_DEV)[:, None, None]

    def inner(left, right):
        scores = jnp.einsum('thd,shd->hts', left.astype(single_float), right.astype(single_float))
        return (scores * table).astype(jnp.bfloat16)

    def forward(prefix_sum, block):
        query_block, key_block, value_block = block
        weights = inner(query_block, key_block)
        attended_output = jnp.einsum('hts,shd->thd', weights.astype(single_float), value_block.astype(single_float))
        attended_output = attended_output + jnp.einsum('web,ebo->weo', query_block.astype(single_float), prefix_sum, precision=highest_precision) * start_weight
        running_state = jnp.einsum('ldg,ldj->dgj', key_block.astype(single_float) * end_weight, value_block.astype(single_float), precision=highest_precision)
        return (block_decay * prefix_sum + running_state, (attended_output, prefix_sum))
    zero_state = jnp.zeros((HEADS, DH, DH), single_float)
    last, (attended_output, prefixes) = lax.scan(forward, zero_state, (qall, kall, vall))
    attended_output = attended_output.reshape(TOKENS, HEADS * DH)
    total = float(HEADS * DH)
    rinv = lax.rsqrt(lax.optimization_barrier(jnp.sum(attended_output * attended_output, axis=1)) / total + 1e-06)[:, None]
    normed = (attended_output * rinv * gain).astype(jnp.bfloat16)
    scaled = out_grad.astype(single_float) * gain
    cross = (lax.optimization_barrier(jnp.sum(scaled * attended_output, axis=1)) / total)[:, None]
    attn_grad = (rinv * scaled - attended_output * (rinv * rinv * rinv * cross)).astype(jnp.bfloat16)
    dall = attn_grad.reshape(shape4)

    def backward(suffix_sum, block):
        query_block, key_block, value_block, decay_bias, prefix_sum = block
        weights = inner(query_block, key_block)
        grad_weights = inner(decay_bias, value_block)
        query_gradient = jnp.einsum('hts,shd->thd', grad_weights.astype(single_float), key_block.astype(single_float))
        query_gradient = query_gradient + jnp.einsum('dmq,msq->dms', decay_bias.astype(single_float), prefix_sum, precision=highest_precision) * start_weight
        key_gradient = jnp.einsum('hts,thd->shd', grad_weights.astype(single_float), query_block.astype(single_float))
        key_gradient = key_gradient + jnp.einsum('noq,ofq->nof', value_block.astype(single_float), suffix_sum, precision=highest_precision) * tail_weight
        value_gradient = jnp.einsum('hts,thd->shd', weights.astype(single_float), decay_bias.astype(single_float))
        value_gradient = value_gradient + jnp.einsum('dyp,ypn->dyn', key_block.astype(single_float), suffix_sum, precision=highest_precision) * tail_weight
        running_state = jnp.einsum('ldg,ldj->dgj', query_block.astype(single_float) * head_weight, decay_bias.astype(single_float), precision=highest_precision)
        grads = (query_gradient.astype(jnp.bfloat16), key_gradient.astype(jnp.bfloat16), value_gradient.astype(jnp.bfloat16))
        return (block_decay * suffix_sum + running_state, grads)
    first, (query_gradient, key_gradient, value_gradient) = lax.scan(backward, zero_state, (qall, kall, vall, dall, prefixes), reverse=True)
    flat = (TOKENS, HEADS * DH)
    return (normed, query_gradient.reshape(flat), key_gradient.reshape(flat), value_gradient.reshape(flat))
```

```python
import functools

import jax
import jax.numpy as jnp
from jax import lax
from jax.experimental import pallas as pl
from jax.experimental.pallas import tpu as pltpu
from jax.sharding import Mesh, PartitionSpec as P

DH = 128
TILE = 128
F32 = jnp.float32
BF16 = jnp.bfloat16
NT = (((1,), (1,)), ((), ()))
TN = (((0,), (0,)), ((), ()))
NN = (((1,), (0,)), ((), ()))
VMEM = pl.BlockSpec(memory_space=pltpu.VMEM)
SMEM = pl.BlockSpec(memory_space=pltpu.SMEM)
PARAMS = pltpu.CompilerParams(vmem_limit_bytes=32 * 2**20)


def dot(left, right, dims):
    return lax.dot_general(left, right, dims, preferred_element_type=F32)


def halves(value):
    high = value.astype(BF16)
    return high, (value - high.astype(F32)).astype(BF16)


def dot_wide(left, right, dims):
    high, low = halves(right)
    return dot(left, high, dims) + dot(left, low, dims)


def rows(count):
    return lax.broadcasted_iota(jnp.int32, (count, DH), 0).astype(F32)


def band(rate, count):
    row = lax.broadcasted_iota(jnp.int32, (TILE, count), 0) + (count - TILE)
    diff = (row - lax.broadcasted_iota(jnp.int32, (TILE, count), 1)).astype(F32)
    return jnp.where(diff >= 0, jnp.exp(-rate * jnp.maximum(diff, 0.0)), 0.0)


def head(h):
    return slice(h * DH, (h + 1) * DH)


def state_kernel(rate_ref, k_ref, v_ref, out_ref):
    count = k_ref.shape[0]
    for h in range(rate_ref.shape[0]):
        weight = jnp.exp(-rate_ref[h] * (count - 1.0 - rows(count)))
        out_ref[head(h), :] = dot_wide(
            k_ref[:, head(h)], v_ref[:, head(h)].astype(F32) * weight, TN
        )


def scan_kernel(reverse, decay_ref, in_ref, out_ref):
    blocks = in_ref.shape[0]
    decay = decay_ref[0]
    total = jnp.zeros(in_ref.shape[1:], F32)
    order = range(blocks - 1, -1, -1) if reverse else range(blocks)
    for b in order:
        out_ref[b] = total
        total = total * decay + in_ref[b]


def inner_kernel(rate_ref, q_ref, k_ref, v_ref, out_ref):
    count = k_ref.shape[0]
    for h in range(rate_ref.shape[0]):
        table = band(rate_ref[h], count)
        for a in range(count // TILE):
            here = slice(a * TILE, (a + 1) * TILE)
            seen = (a + 1) * TILE
            scores = dot(q_ref[here, head(h)], k_ref[:seen, head(h)], NT)
            weights = (scores * table[:, count - seen :]).astype(BF16)
            out_ref[here, head(h)] = dot(weights, v_ref[:seen, head(h)], NN)


def attend_kernel(rate_ref, q_ref, g_ref, gain_ref, inner_ref, prefix_ref, att_ref, sums_ref):
    count = q_ref.shape[0]
    squares = jnp.zeros((count, DH), F32)
    crossing = jnp.zeros((count, DH), F32)
    for h in range(rate_ref.shape[0]):
        weight = jnp.exp(-rate_ref[h] * (rows(count) + 1.0))
        attended = (
            inner_ref[:, head(h)]
            + dot_wide(q_ref[:, head(h)], prefix_ref[head(h), :], NN) * weight
        )
        att_ref[:, head(h)] = attended
        scaled = g_ref[:, head(h)].astype(F32) * gain_ref[:, head(h)]
        squares += attended * attended
        crossing += scaled * attended
    ones = jnp.ones((8, DH), BF16)
    for index, part in enumerate((squares, crossing)):
        high, low = halves(part)
        sums_ref[index : index + 1, :] = (dot(ones, high, NT) + dot(ones, low, NT))[:1]


def norm_kernel(
    total, rate_ref, q_ref, g_ref, gain_ref, att_ref, sums_ref, grad_ref, state_ref, normed_ref
):
    count = q_ref.shape[0]
    ones = jnp.ones((sums_ref.shape[0], DH), F32)

    def spread(index):
        return lax.dot_general(
            sums_ref[:, index, :], ones, TN, precision=lax.Precision.HIGHEST,
            preferred_element_type=F32,
        )

    rinv = lax.rsqrt(spread(0) / total + 1e-06)
    cross = spread(1) / total
    factor = rinv * rinv * rinv * cross
    for h in range(rate_ref.shape[0]):
        weight = jnp.exp(-rate_ref[h] * rows(count))
        attended = att_ref[:, head(h)]
        gain = gain_ref[:, head(h)]
        scaled = g_ref[:, head(h)].astype(F32) * gain
        grad = (rinv * scaled - attended * factor).astype(BF16)
        grad_ref[:, head(h)] = grad
        normed_ref[:, head(h)] = (attended * rinv * gain).astype(BF16)
        state_ref[head(h), :] = dot_wide(q_ref[:, head(h)], grad.astype(F32) * weight, TN)


def back_kernel(
    rate_ref, q_ref, k_ref, v_ref, d_ref, prefix_ref, dq_ref, dk_ref, dv_ref
):
    count = q_ref.shape[0]
    for h in range(rate_ref.shape[0]):
        table = band(rate_ref[h], count)
        weight = jnp.exp(-rate_ref[h] * (rows(count) + 1.0))
        past = dot_wide(d_ref[:, head(h)], prefix_ref[head(h), :], NT) * weight
        for a in range(count // TILE):
            here = slice(a * TILE, (a + 1) * TILE)
            seen = (a + 1) * TILE
            part = table[:, count - seen :]
            q, d = q_ref[here, head(h)], d_ref[here, head(h)]
            weights = (dot(q, k_ref[:seen, head(h)], NT) * part).astype(BF16)
            grads = (dot(d, v_ref[:seen, head(h)], NT) * part).astype(BF16)
            dq_ref[here, head(h)] = (
                dot(grads, k_ref[:seen, head(h)], NN) + past[here, :]
            ).astype(BF16)
            dk, dv = dot(grads, q, TN), dot(weights, d, TN)
            if a:
                before = slice(0, a * TILE)
                dk_ref[before, head(h)] += dk[before, :]
                dv_ref[before, head(h)] += dv[before, :]
            dk_ref[here, head(h)] = dk[here, :]
            dv_ref[here, head(h)] = dv[here, :]


def final_kernel(rate_ref, k_ref, v_ref, suffix_ref, dk_ref, dv_ref, kout_ref, vout_ref):
    count = k_ref.shape[0]
    for h in range(rate_ref.shape[0]):
        weight = jnp.exp(-rate_ref[h] * (count - rows(count)))
        suffix = suffix_ref[head(h), :]
        kout_ref[:, head(h)] = (
            dk_ref[:, head(h)] + dot_wide(v_ref[:, head(h)], suffix, NT) * weight
        ).astype(BF16)
        vout_ref[:, head(h)] = (
            dv_ref[:, head(h)] + dot_wide(k_ref[:, head(h)], suffix, NN) * weight
        ).astype(BF16)


def call(kernel, shapes, specs, *args, name, flops=0, size=0):
    return pl.pallas_call(
        kernel,
        out_shape=shapes,
        in_specs=specs,
        out_specs=jax.tree.map(lambda _: VMEM, shapes),
        compiler_params=PARAMS,
        cost_estimate=pl.CostEstimate(flops=flops, bytes_accessed=size, transcendentals=0),
        name=name,
    )(*args)


def scan(state, decay, reverse):
    axes = ("y", "x")
    blocks = lax.axis_size(axes)
    pieces = state.reshape(blocks, -1, DH)
    mine = lax.all_to_all(pieces, axes, 0, 0, tiled=True)
    owner = lax.axis_index(axes) * decay.shape[0] // blocks
    rate = lax.dynamic_slice(decay, (owner,), (1,))
    sums = call(
        functools.partial(scan_kernel, reverse),
        jax.ShapeDtypeStruct(mine.shape, F32),
        [SMEM, VMEM],
        rate, mine,
        name="scan",
        size=2 * mine.size * 4,
    )
    return lax.all_to_all(sums, axes, 0, 0, tiled=True).reshape(state.shape)


def local(queries, keys, values, out_grad, decay_rate, gain):
    count, width = queries.shape
    heads = decay_rate.shape[0]
    shape = jax.ShapeDtypeStruct
    gain = gain[None, :]
    decay = jnp.exp(-decay_rate * count)
    pair = 2 * count * count * DH * heads
    wide = 2 * count * DH * DH * heads * 2
    state = call(
        state_kernel, shape((width, DH), F32), [SMEM, VMEM, VMEM],
        decay_rate, keys, values, name="state", flops=wide, size=4 * count * width,
    )
    prefix = scan(state, decay, False)
    inner = call(
        inner_kernel, shape((count, width), F32), [SMEM] + [VMEM] * 3,
        decay_rate, queries, keys, values, name="inner", flops=2 * pair, size=10 * count * width,
    )
    attended, sums = call(
        attend_kernel,
        (shape((count, width), F32), shape((2, count), F32)),
        [SMEM] + [VMEM] * 5,
        decay_rate, queries, out_grad, gain, inner, prefix,
        name="attend", flops=wide, size=12 * count * width,
    )
    sums = lax.all_gather(sums[None], ("z", "c"), axis=0, tiled=True)
    total = float(heads * lax.axis_size(("z", "c")) * DH)
    grad, state, normed = call(
        functools.partial(norm_kernel, total),
        (shape((count, width), BF16), shape((width, DH), F32), shape((count, width), BF16)),
        [SMEM] + [VMEM] * 5,
        decay_rate, queries, out_grad, gain, attended, sums,
        name="norm", flops=wide, size=12 * count * width,
    )
    suffix = scan(state, decay, True)
    dq, dk, dv = call(
        back_kernel,
        (shape((count, width), BF16), shape((count, width), F32), shape((count, width), F32)),
        [SMEM] + [VMEM] * 5,
        decay_rate, queries, keys, values, grad, prefix,
        name="back", flops=5 * pair, size=18 * count * width,
    )
    dk, dv = call(
        final_kernel,
        (shape((count, width), BF16), shape((count, width), BF16)),
        [SMEM] + [VMEM] * 5,
        decay_rate, keys, values, suffix, dk, dv,
        name="final", flops=2 * wide, size=16 * count * width,
    )
    return normed, dq, dk, dv


def solution(mesh):
    fine = Mesh(mesh.devices.reshape(8, 4, 8, 2), ("y", "x", "z", "c"))
    ctx, head_axes = ("y", "x"), ("z", "c")
    tokens = P(ctx, head_axes)
    return jax.shard_map(
        local,
        mesh=fine,
        in_specs=(tokens,) * 4 + (P(head_axes),) * 2,
        out_specs=(tokens,) * 4,
        check_vma=False,
    )
```

```python
import functools

import jax
import jax.numpy as jnp
from jax import lax
from jax.experimental import pallas as pl
from jax.experimental.pallas import tpu as pltpu
from jax.sharding import Mesh, PartitionSpec as P

DH = 128
TILE = 128
F32 = jnp.float32
BF16 = jnp.bfloat16
NT = (((1,), (1,)), ((), ()))
TN = (((0,), (0,)), ((), ()))
NN = (((1,), (0,)), ((), ()))
VMEM = pl.BlockSpec(memory_space=pltpu.VMEM)
SMEM = pl.BlockSpec(memory_space=pltpu.SMEM)
ANY = pl.BlockSpec(memory_space=pl.ANY)


def dot(left, right, dims):
    return lax.dot_general(left, right, dims, preferred_element_type=F32)


def halves(value):
    high = value.astype(BF16)
    return high, (value - high.astype(F32)).astype(BF16)


def dot_wide(left, right):
    return dot(
        jnp.concatenate([left, left], axis=1), jnp.concatenate(halves(right), axis=0), NN
    )


def rows(count):
    return lax.broadcasted_iota(jnp.int32, (count, DH), 0).astype(F32)


def band(rate, count):
    row = lax.broadcasted_iota(jnp.int32, (TILE, count), 0) + (count - TILE)
    diff = (row - lax.broadcasted_iota(jnp.int32, (TILE, count), 1)).astype(F32)
    return jnp.where(diff >= 0, jnp.exp(-rate * jnp.maximum(diff, 0.0)), 0.0)


def head(h):
    return slice(h * DH, (h + 1) * DH)


def diagonal():
    return lax.broadcasted_iota(jnp.int32, (TILE, TILE), 0) == lax.broadcasted_iota(
        jnp.int32, (TILE, TILE), 1
    )


def to_rows(part):
    sums = jnp.sum(part, axis=1, keepdims=True)
    mask = diagonal()
    return [
        jnp.sum(jnp.where(mask, sums[a * TILE : (a + 1) * TILE, :], 0.0), axis=0, keepdims=True)
        for a in range(part.shape[0] // TILE)
    ]


def to_columns(table, first, tiles):
    mask = diagonal()
    return jnp.concatenate(
        [
            jnp.sum(jnp.where(mask, table[a : a + 1, :], 0.0), axis=1, keepdims=True)
            for a in range(first, first + tiles)
        ],
        axis=0,
    )


def state_kernel(rate_hbm, k_hbm, v_hbm, out_ref, rate_ref, k_ref, v_ref, sems):
    count = k_ref.shape[0]
    copies = [
        pltpu.make_async_copy(rate_hbm, rate_ref, sems.at[0]),
        pltpu.make_async_copy(k_hbm, k_ref, sems.at[1]),
        pltpu.make_async_copy(v_hbm, v_ref, sems.at[2]),
    ]
    for copy in copies:
        copy.start()
    back = count - 1.0 - rows(count)
    for copy in copies:
        copy.wait()
    for h in range(rate_ref.shape[0]):
        weight = jnp.exp(-rate_ref[h] * back)
        both = jnp.concatenate(halves(v_ref[:, head(h)].astype(F32) * weight), axis=1)
        sums = dot(k_ref[:, head(h)], both, TN)
        out_ref[head(h), :] = sums[:, :DH] + sums[:, DH:]


def scan_kernel(reverse, decay_ref, in_ref, out_ref):
    blocks = in_ref.shape[0]
    decay = decay_ref[...]
    total = jnp.zeros(in_ref.shape[1:], F32)
    order = range(blocks - 1, -1, -1) if reverse else range(blocks)
    for b in order:
        out_ref[b] = total
        total = total * decay + in_ref[b]


def inner_kernel(rate_ref, q_ref, k_ref, v_ref, out_ref, start_ref, turned_ref):
    count = k_ref.shape[0]
    for h in range(rate_ref.shape[0]):
        rate = rate_ref[h]
        table = band(rate, count)
        start_ref[:, head(h)] = jnp.exp(-rate * (rows(count) + 1.0))
        scaled = q_ref[:, head(h)].astype(F32) * jnp.exp(-rate * rows(count))
        high, low = halves(scaled.T)
        turned_ref[2 * h * DH : (2 * h + 1) * DH, :] = high
        turned_ref[(2 * h + 1) * DH : (2 * h + 2) * DH, :] = low
        for a in range(count // TILE):
            here = slice(a * TILE, (a + 1) * TILE)
            seen = (a + 1) * TILE
            scores = dot(q_ref[here, head(h)], k_ref[:seen, head(h)], NT)
            weights = (scores * table[:, count - seen :]).astype(BF16)
            out_ref[here, head(h)] = dot(weights, v_ref[:seen, head(h)], NN)


def attend_kernel(q_ref, g_ref, gain_ref, inner_ref, start_ref, prefix_ref, att_ref, sums_ref):
    count, width = q_ref.shape
    squares = jnp.zeros((count, DH), F32)
    crossing = jnp.zeros((count, DH), F32)
    for h in range(width // DH):
        attended = (
            inner_ref[:, head(h)]
            + dot_wide(q_ref[:, head(h)], prefix_ref[head(h), :]) * start_ref[:, head(h)]
        )
        att_ref[:, head(h)] = attended
        scaled = g_ref[:, head(h)].astype(F32) * gain_ref[:, head(h)]
        squares += attended * attended
        crossing += scaled * attended
    both = jnp.concatenate(to_rows(squares) + to_rows(crossing), axis=0)
    for j in range(sums_ref.shape[0]):
        sums_ref[j] = both


def norm_scales(total, sums_ref):
    tiles = sums_ref.shape[1] // 2
    table = jnp.sum(sums_ref[...], axis=0) / total
    rinv = lax.rsqrt(table[:tiles, :] + 1e-06)
    factor = rinv * rinv * rinv * table[tiles:, :]
    return rinv, factor, tiles


def norm_kernel(total, g_ref, gain_ref, att_ref, turned_ref, sums_ref, grad_ref, state_ref):
    rinv, factor, tiles = norm_scales(total, sums_ref)
    rinv, factor = to_columns(rinv, 0, tiles), to_columns(factor, 0, tiles)
    for h in range(g_ref.shape[1] // DH):
        scaled = g_ref[:, head(h)].astype(F32) * gain_ref[:, head(h)]
        grad = (rinv * scaled - att_ref[:, head(h)] * factor).astype(BF16)
        grad_ref[:, head(h)] = grad
        sums = dot(turned_ref[2 * h * DH : (2 * h + 2) * DH, :], grad, NN)
        state_ref[head(h), :] = sums[:DH, :] + sums[DH:, :]


def back_kernel(
    total, rate_ref, q_ref, k_ref, v_ref, d_ref, prefix_ref, start_ref, att_ref, gain_ref, sums_ref,
    normed_ref, dq_ref, dk_ref, dv_ref, tail_ref,
):
    count = q_ref.shape[0]
    rinv, _, tiles = norm_scales(total, sums_ref)
    rinv = to_columns(rinv, 0, tiles)
    for h in range(rate_ref.shape[0]):
        normed_ref[:, head(h)] = (att_ref[:, head(h)] * rinv * gain_ref[:, head(h)]).astype(BF16)
        table = band(rate_ref[h], count)
        tail_ref[:, head(h)] = jnp.exp(-rate_ref[h] * (count - rows(count)))
        past = dot_wide(d_ref[:, head(h)], prefix_ref[head(h), :].T) * start_ref[:, head(h)]
        for a in range(count // TILE):
            here = slice(a * TILE, (a + 1) * TILE)
            seen = (a + 1) * TILE
            part = table[:, count - seen :]
            q, d = q_ref[here, head(h)], d_ref[here, head(h)]
            weights = (dot(q, k_ref[:seen, head(h)], NT) * part).astype(BF16)
            grads = (dot(d, v_ref[:seen, head(h)], NT) * part).astype(BF16)
            dq_ref[here, head(h)] = (
                dot(grads, k_ref[:seen, head(h)], NN) + past[here, :]
            ).astype(BF16)
            dk, dv = dot(grads, q, TN), dot(weights, d, TN)
            if a:
                before = slice(0, a * TILE)
                dk_ref[before, head(h)] += dk[before, :]
                dv_ref[before, head(h)] += dv[before, :]
            dk_ref[here, head(h)] = dk[here, :]
            dv_ref[here, head(h)] = dv[here, :]


def final_kernel(
    k_ref, v_ref, suffix_ref, dk_ref, dv_ref, tail_ref, kout_hbm, vout_hbm, kout_ref, vout_ref, sems
):
    heads = k_ref.shape[1] // DH
    copies = []
    for h in range(heads):
        tail = tail_ref[:, head(h)]
        suffix = suffix_ref[head(h), :]
        kout_ref[:, head(h)] = (
            dk_ref[:, head(h)] + dot_wide(v_ref[:, head(h)], suffix.T) * tail
        ).astype(BF16)
        vout_ref[:, head(h)] = (
            dv_ref[:, head(h)] + dot_wide(k_ref[:, head(h)], suffix) * tail
        ).astype(BF16)
        for index, (held, out) in enumerate(((kout_ref, kout_hbm), (vout_ref, vout_hbm))):
            copy = pltpu.make_async_copy(
                held.at[:, head(h)], out.at[:, head(h)], sems.at[2 * h + index]
            )
            copy.start()
            copies.append(copy)
    for copy in copies:
        copy.wait()


def call(kernel, shapes, specs, *args, name, flops, size, mib=8, out_specs=None, scratch=()):
    return pl.pallas_call(
        kernel,
        out_shape=shapes,
        in_specs=specs,
        out_specs=out_specs or jax.tree.map(lambda _: VMEM, shapes),
        scratch_shapes=scratch,
        compiler_params=pltpu.CompilerParams(vmem_limit_bytes=mib * 2**20),
        cost_estimate=pl.CostEstimate(flops=flops, bytes_accessed=size, transcendentals=0),
        name=name,
    )(*args)


def scan(state, decay, reverse):
    axes = ("y", "x")
    blocks = lax.axis_size(axes)
    pieces = state.reshape(blocks, -1, DH)
    mine = lax.all_to_all(pieces, axes, 0, 0, tiled=True)
    sums = call(
        functools.partial(scan_kernel, reverse),
        jax.ShapeDtypeStruct(mine.shape, F32),
        [VMEM, VMEM],
        decay, mine,
        name="scan", flops=2 * mine.size, size=2 * mine.size * 4, mib=2,
    )
    return lax.all_to_all(sums, axes, 0, 0, tiled=True).reshape(state.shape)


def local(queries, keys, values, out_grad, decay_rate, gain):
    count, width = queries.shape
    heads = decay_rate.shape[0]
    ctx, head_axes = ("y", "x"), ("z", "c")
    shape = jax.ShapeDtypeStruct
    whole32, whole16 = shape((count, width), F32), shape((count, width), BF16)
    state_shape = shape((width, DH), F32)
    gain = gain[None, :]
    owner = lax.axis_index(ctx) * heads // lax.axis_size(ctx)
    decay = jnp.exp(-lax.dynamic_slice(decay_rate, (owner,), (1,)) * count)
    decay = jnp.broadcast_to(decay[None, :], (1, DH))
    pair = 2 * count * count * DH * heads
    wide = 4 * count * DH * DH * heads
    unit = count * width
    state = call(
        state_kernel, state_shape, [ANY] * 3, decay_rate, keys, values,
        name="state", flops=wide, size=4 * unit, mib=48,
        scratch=[
            pltpu.SMEM((heads,), F32),
            pltpu.VMEM((count, width), BF16),
            pltpu.VMEM((count, width), BF16),
            pltpu.SemaphoreType.DMA((3,)),
        ],
    )
    prefix = scan(state, decay, False)
    inner, start, turned = call(
        inner_kernel, (whole32, whole32, shape((2 * width, count), BF16)), [SMEM] + [VMEM] * 3,
        decay_rate, queries, keys, values,
        name="inner", flops=2 * pair, size=18 * unit, mib=12,
    )
    groups = lax.axis_size(head_axes)
    attended, sums = call(
        attend_kernel, (whole32, shape((groups, 2 * count // TILE, TILE), F32)), [VMEM] * 6,
        queries, out_grad, gain, inner, start, prefix,
        name="attend", flops=wide, size=16 * unit,
    )
    sums = lax.all_to_all(sums, head_axes, 0, 0, tiled=True)
    total = float(heads * groups * DH)
    grad, state = call(
        functools.partial(norm_kernel, total), (whole16, state_shape), [VMEM] * 5,
        out_grad, gain, attended, turned, sums,
        name="norm", flops=wide, size=12 * unit,
    )
    suffix = scan(state, decay, True)
    normed, dq, dk, dv, tail = call(
        functools.partial(back_kernel, total), (whole16, whole16, whole32, whole32, whole32),
        [SMEM] + [VMEM] * 9,
        decay_rate, queries, keys, values, grad, prefix, start, attended, gain, sums,
        name="back", flops=5 * pair, size=32 * unit, mib=16,
    )
    dk, dv = call(
        final_kernel, (whole16, whole16), [VMEM] * 6,
        keys, values, suffix, dk, dv, tail,
        name="final", flops=2 * wide, size=20 * unit, out_specs=(ANY, ANY),
        scratch=[
            pltpu.VMEM((count, width), BF16),
            pltpu.VMEM((count, width), BF16),
            pltpu.SemaphoreType.DMA((2 * heads,)),
        ],
    )
    return normed, dq, dk, dv


def solution(mesh):
    fine = Mesh(mesh.devices.reshape(8, 4, 8, 2), ("y", "x", "z", "c"))
    ctx, head_axes = ("y", "x"), ("z", "c")
    tokens = P(ctx, head_axes)
    return jax.shard_map(
        local,
        mesh=fine,
        in_specs=(tokens,) * 4 + (P(head_axes),) * 2,
        out_specs=(tokens,) * 4,
        check_vma=False,
    )
```

```python
import functools

import jax
import jax.numpy as jnp
from jax import lax
from jax.experimental import pallas as pl
from jax.experimental.pallas import tpu as pltpu
from jax.sharding import Mesh, PartitionSpec as P

DH = 128
TILE = 128
F32 = jnp.float32
BF16 = jnp.bfloat16
NT = (((1,), (1,)), ((), ()))
TN = (((0,), (0,)), ((), ()))
NN = (((1,), (0,)), ((), ()))
VMEM = pl.BlockSpec(memory_space=pltpu.VMEM)
SMEM = pl.BlockSpec(memory_space=pltpu.SMEM)
ANY = pl.BlockSpec(memory_space=pl.ANY)


def dot(left, right, dims):
    return lax.dot_general(left, right, dims, preferred_element_type=F32)


def halves(value):
    high = value.astype(BF16)
    return high, (value - high.astype(F32)).astype(BF16)


def dot_wide(left, right):
    return dot(
        jnp.concatenate([left, left], axis=1), jnp.concatenate(halves(right), axis=0), NN
    )


def rising(rate, count):
    step = lax.broadcasted_iota(jnp.int32, (8, DH), 0).astype(F32)
    table, size = jnp.exp(-rate * step), 8
    while size < count:
        table = jnp.concatenate([table, table * jnp.exp(-rate * size)], axis=0)
        size *= 2
    return table


def falling(rate, count):
    step = 8.0 - lax.broadcasted_iota(jnp.int32, (8, DH), 0).astype(F32)
    table, size = jnp.exp(-rate * step), 8
    while size < count:
        table = jnp.concatenate([table * jnp.exp(-rate * size), table], axis=0)
        size *= 2
    return table


def band(rate, count):
    row = lax.broadcasted_iota(jnp.int32, (TILE, count), 0) + (count - TILE)
    diff = (row - lax.broadcasted_iota(jnp.int32, (TILE, count), 1)).astype(F32)
    wide = jnp.concatenate([rate] * (count // DH), axis=1)
    return jnp.where(diff >= 0, jnp.exp(-wide * jnp.maximum(diff, 0.0)), 0.0)


def fetch(pairs, sems):
    copies = [
        pltpu.make_async_copy(far, near, sems.at[i]) for i, (far, near) in enumerate(pairs)
    ]
    for copy in copies:
        copy.start()
    return copies


def wait(copies):
    for copy in copies:
        copy.wait()


def head(h):
    return slice(h * DH, (h + 1) * DH)


def diagonal():
    return lax.broadcasted_iota(jnp.int32, (TILE, TILE), 0) == lax.broadcasted_iota(
        jnp.int32, (TILE, TILE), 1
    )


def to_rows(part):
    sums = jnp.sum(part, axis=1, keepdims=True)
    mask = diagonal()
    return [
        jnp.sum(jnp.where(mask, sums[a * TILE : (a + 1) * TILE, :], 0.0), axis=0, keepdims=True)
        for a in range(part.shape[0] // TILE)
    ]


def to_columns(table, first, tiles):
    mask = diagonal()
    return jnp.concatenate(
        [
            jnp.sum(jnp.where(mask, table[a : a + 1, :], 0.0), axis=1, keepdims=True)
            for a in range(first, first + tiles)
        ],
        axis=0,
    )


def state_kernel(rate_hbm, k_hbm, v_hbm, out_ref, rate_ref, k_ref, v_ref, sems):
    count = k_ref.shape[0]
    copies = fetch(((rate_hbm, rate_ref), (k_hbm, k_ref), (v_hbm, v_ref)), sems)
    wait(copies)
    for h in range(rate_ref.shape[0]):
        rate = jnp.full((1, DH), rate_ref[h], F32)
        weight = falling(rate, count) * jnp.exp(rate)
        both = jnp.concatenate(halves(v_ref[:, head(h)].astype(F32) * weight), axis=1)
        sums = dot(k_ref[:, head(h)], both, TN)
        out_ref[head(h), :] = sums[:, :DH] + sums[:, DH:]


def scan_kernel(reverse, decay_ref, in_ref, out_ref):
    blocks = in_ref.shape[0]
    decay = decay_ref[...]
    total = jnp.zeros(in_ref.shape[1:], F32)
    order = range(blocks - 1, -1, -1) if reverse else range(blocks)
    for b in order:
        out_ref[b] = total
        total = total * decay + in_ref[b]


def inner_kernel(aux_ref, q_hbm, k_hbm, v_hbm, out_ref, q_ref, k_ref, v_ref, sems):
    count, width = k_ref.shape
    wait(fetch(((q_hbm, q_ref), (k_hbm, k_ref), (v_hbm, v_ref)), sems))
    for h in range(width // DH):
        table = band(aux_ref[1:2, head(h)], count)
        for a in range(count // TILE):
            here = slice(a * TILE, (a + 1) * TILE)
            seen = (a + 1) * TILE
            scores = dot(q_ref[here, head(h)], k_ref[:seen, head(h)], NT)
            weights = (scores * table[:, count - seen :]).astype(BF16)
            out_ref[here, head(h)] = dot(weights, v_ref[:seen, head(h)], NN)


def attend_kernel(aux_ref, q_ref, g_ref, inner_ref, prefix_ref, att_ref, sums_ref):
    count, width = q_ref.shape
    squares = jnp.zeros((count, DH), F32)
    crossing = jnp.zeros((count, DH), F32)
    for h in range(width // DH):
        rate = aux_ref[1:2, head(h)]
        weight = rising(rate, count) * jnp.exp(-rate)
        attended = (
            inner_ref[:, head(h)] + dot_wide(q_ref[:, head(h)], prefix_ref[head(h), :]) * weight
        )
        att_ref[:, head(h)] = attended
        squares += attended * attended
        crossing += g_ref[:, head(h)].astype(F32) * aux_ref[0:1, head(h)] * attended
    both = jnp.concatenate(to_rows(squares) + to_rows(crossing), axis=0)
    for j in range(sums_ref.shape[0]):
        sums_ref[j] = both


def turn_kernel(q_hbm, out_ref, q_ref, sems):
    wait(fetch(((q_hbm, q_ref),), sems))
    for h in range(q_ref.shape[1] // DH):
        out_ref[head(h), :] = q_ref[:, head(h)].T


def norm_scales(total, sums_ref):
    tiles = sums_ref.shape[1] // 2
    table = jnp.sum(sums_ref[...], axis=0) / total
    rinv = lax.rsqrt(table[:tiles, :] + 1e-06)
    factor = rinv * rinv * rinv * table[tiles:, :]
    return rinv, factor, tiles


def norm_kernel(
    total, aux_ref, turned_ref, g_ref, att_ref, sums_ref, grad_ref, state_ref
):
    count, width = g_ref.shape
    rinv, factor, tiles = norm_scales(total, sums_ref)
    rinv, factor = to_columns(rinv, 0, tiles), to_columns(factor, 0, tiles)
    for h in range(width // DH):
        scaled = g_ref[:, head(h)].astype(F32) * aux_ref[0:1, head(h)]
        grad = (rinv * scaled - att_ref[:, head(h)] * factor).astype(BF16)
        grad_ref[:, head(h)] = grad
        weight = rising(aux_ref[1:2, head(h)], count)
        both = jnp.concatenate(halves(grad.astype(F32) * weight), axis=1)
        sums = dot(turned_ref[head(h), :], both, NN)
        state_ref[head(h), :] = sums[:, :DH] + sums[:, DH:]


def query_kernel(
    total, aux_ref, k_hbm, v_hbm, d_ref, prefix_ref, att_ref, sums_ref,
    normed_ref, dq_ref, k_ref, v_ref, sems,
):
    count, width = k_ref.shape
    copies = fetch(((k_hbm, k_ref), (v_hbm, v_ref)), sems)
    rinv, _, tiles = norm_scales(total, sums_ref)
    rinv = to_columns(rinv, 0, tiles)
    for h in range(width // DH):
        normed_ref[:, head(h)] = (att_ref[:, head(h)] * rinv * aux_ref[0:1, head(h)]).astype(BF16)
    wait(copies)
    for h in range(width // DH):
        rate = aux_ref[1:2, head(h)]
        table = band(rate, count)
        weight = rising(rate, count) * jnp.exp(-rate)
        past = dot_wide(d_ref[:, head(h)], prefix_ref[head(h), :].T) * weight
        for a in range(count // TILE):
            here = slice(a * TILE, (a + 1) * TILE)
            seen = (a + 1) * TILE
            scores = dot(d_ref[here, head(h)], v_ref[:seen, head(h)], NT)
            grads = (scores * table[:, count - seen :]).astype(BF16)
            dq_ref[here, head(h)] = (
                dot(grads, k_ref[:seen, head(h)], NN) + past[here, :]
            ).astype(BF16)


def back_kernel(aux_ref, q_hbm, k_hbm, v_hbm, d_ref, dk_ref, dv_ref, q_ref, k_ref, v_ref, sems):
    count, width = q_ref.shape
    wait(fetch(((q_hbm, q_ref), (k_hbm, k_ref), (v_hbm, v_ref)), sems))
    for h in range(width // DH):
        table = band(aux_ref[1:2, head(h)], count)
        for a in range(count // TILE):
            here = slice(a * TILE, (a + 1) * TILE)
            seen = (a + 1) * TILE
            part = table[:, count - seen :]
            q, d = q_ref[here, head(h)], d_ref[here, head(h)]
            weights = (dot(q, k_ref[:seen, head(h)], NT) * part).astype(BF16)
            grads = (dot(d, v_ref[:seen, head(h)], NT) * part).astype(BF16)
            dk, dv = dot(grads, q, TN), dot(weights, d, TN)
            if a:
                before = slice(0, a * TILE)
                dk_ref[before, head(h)] += dk[before, :]
                dv_ref[before, head(h)] += dv[before, :]
            dk_ref[here, head(h)] = dk[here, :]
            dv_ref[here, head(h)] = dv[here, :]


def final_kernel(
    aux_ref, k_ref, v_ref, suffix_ref, dk_ref, dv_ref, kout_hbm, vout_hbm, kout_ref, vout_ref, sems
):
    count, width = k_ref.shape
    copies = []
    for h in range(width // DH):
        tail = falling(aux_ref[1:2, head(h)], count)
        suffix = suffix_ref[head(h), :]
        kout_ref[:, head(h)] = (
            dk_ref[:, head(h)] + dot_wide(v_ref[:, head(h)], suffix.T) * tail
        ).astype(BF16)
        vout_ref[:, head(h)] = (
            dv_ref[:, head(h)] + dot_wide(k_ref[:, head(h)], suffix) * tail
        ).astype(BF16)
        for index, (held, out) in enumerate(((kout_ref, kout_hbm), (vout_ref, vout_hbm))):
            copy = pltpu.make_async_copy(
                held.at[:, head(h)], out.at[:, head(h)], sems.at[2 * h + index]
            )
            copy.start()
            copies.append(copy)
    wait(copies)


def call(kernel, shapes, specs, *args, name, flops, size, mib=8, out_specs=None, scratch=()):
    return pl.pallas_call(
        kernel,
        out_shape=shapes,
        in_specs=specs,
        out_specs=out_specs or tuple(VMEM for _ in shapes),
        scratch_shapes=scratch,
        compiler_params=pltpu.CompilerParams(vmem_limit_bytes=mib * 2**20),
        cost_estimate=pl.CostEstimate(flops=flops, bytes_accessed=size, transcendentals=0),
        name=name,
    )(*args)


def scan(state, decay, reverse):
    axes = ("y", "x")
    blocks = lax.axis_size(axes)
    pieces = state.reshape(blocks, -1, DH)
    mine = lax.all_to_all(pieces, axes, 0, 0, tiled=True)
    (sums,) = call(
        functools.partial(scan_kernel, reverse),
        (jax.ShapeDtypeStruct(mine.shape, F32),),
        [VMEM, VMEM],
        decay, mine,
        name="scan", flops=2 * mine.size, size=2 * mine.size * 4, mib=2,
    )
    return lax.all_to_all(sums, axes, 0, 0, tiled=True).reshape(state.shape)


def local(queries, keys, values, out_grad, decay_rate, gain):
    count, width = queries.shape
    heads = decay_rate.shape[0]
    ctx, head_axes = ("y", "x"), ("z", "c")
    shape = jax.ShapeDtypeStruct
    whole, state_shape = (count, width), (width, DH)
    aux = jnp.stack([gain, jnp.repeat(decay_rate, DH)])
    owner = lax.axis_index(ctx) * heads // lax.axis_size(ctx)
    decay = jnp.exp(-lax.dynamic_slice(decay_rate, (owner,), (1,)) * count)
    decay = jnp.broadcast_to(decay[None, :], (1, DH))
    pair = 2 * count * count * DH * heads
    wide = 4 * count * DH * DH * heads
    unit = count * width
    far_rate, far_q, far_k, far_v = (
        pltpu.with_memory_space_constraint(array, pltpu.HBM)
        for array in (decay_rate, queries, keys, values)
    )
    block = pltpu.VMEM(whole, BF16)
    (state,) = call(
        state_kernel, (shape(state_shape, F32),), [ANY] * 3, far_rate, far_k, far_v,
        name="state", flops=wide, size=4 * unit,
        scratch=[pltpu.SMEM((heads,), F32), block, block, pltpu.SemaphoreType.DMA((3,))],
    )
    prefix = scan(state, decay, False)
    (inner,) = call(
        inner_kernel, (shape(whole, F32),), [VMEM] + [ANY] * 3, aux, far_q, far_k, far_v,
        name="inner", flops=2 * pair, size=10 * unit,
        scratch=[block, block, block, pltpu.SemaphoreType.DMA((3,))],
    )
    groups = lax.axis_size(head_axes)
    attended, sums = call(
        attend_kernel,
        (shape(whole, F32), shape((groups, 2 * count // TILE, TILE), F32)), [VMEM] * 5,
        aux, queries, out_grad, inner, prefix,
        name="attend", flops=wide, size=12 * unit,
    )
    sums = lax.all_to_all(sums, head_axes, 0, 0, tiled=True)
    (turned,) = call(
        turn_kernel, (shape((width, count), BF16),), [ANY], far_q,
        name="turn", flops=pair, size=4 * unit, mib=4,
        scratch=[block, pltpu.SemaphoreType.DMA((1,))],
    )
    total = float(heads * groups * DH)
    grad, state = call(
        functools.partial(norm_kernel, total),
        (shape(whole, BF16), shape(state_shape, F32)), [VMEM] * 5,
        aux, turned, out_grad, attended, sums,
        name="norm", flops=wide, size=12 * unit,
    )
    normed, dq = call(
        functools.partial(query_kernel, total),
        (shape(whole, BF16), shape(whole, BF16)), [VMEM] + [ANY] * 2 + [VMEM] * 4,
        aux, far_k, far_v, grad, prefix, attended, sums,
        name="query", flops=2 * pair, size=16 * unit,
        scratch=[block, block, pltpu.SemaphoreType.DMA((2,))],
    )
    decay, normed, dq = lax.optimization_barrier((decay, normed, dq))
    suffix = scan(state, decay, True)
    dk, dv = call(
        back_kernel, (shape(whole, F32), shape(whole, F32)), [VMEM] + [ANY] * 3 + [VMEM],
        aux, far_q, far_k, far_v, grad,
        name="back", flops=4 * pair, size=16 * unit,
        scratch=[block, block, block, pltpu.SemaphoreType.DMA((3,))],
    )
    dk, dv = call(
        final_kernel, (shape(whole, BF16), shape(whole, BF16)), [VMEM] * 6,
        aux, keys, values, suffix, dk, dv,
        name="final", flops=2 * wide, size=20 * unit, out_specs=(ANY, ANY),
        scratch=[block, block, pltpu.SemaphoreType.DMA((2 * heads,))],
    )
    return normed, dq, dk, dv


def solution(mesh):
    fine = Mesh(mesh.devices.reshape(8, 4, 8, 2), ("y", "x", "z", "c"))
    ctx, head_axes = ("y", "x"), ("z", "c")
    tokens = P(ctx, head_axes)
    return jax.shard_map(
        local,
        mesh=fine,
        in_specs=(tokens,) * 4 + (P(head_axes),) * 2,
        out_specs=(tokens,) * 4,
        check_vma=False,
    )
```

```python
import functools

import jax
import jax.numpy as jnp
from jax import lax
from jax.experimental import pallas as pl
from jax.experimental.pallas import tpu as pltpu
from jax.sharding import Mesh, PartitionSpec as P

DH = 128
TILE = 128
F32 = jnp.float32
BF16 = jnp.bfloat16
NT = (((1,), (1,)), ((), ()))
TN = (((0,), (0,)), ((), ()))
NN = (((1,), (0,)), ((), ()))
VMEM = pl.BlockSpec(memory_space=pltpu.VMEM)
SMEM = pl.BlockSpec(memory_space=pltpu.SMEM)
ANY = pl.BlockSpec(memory_space=pl.ANY)


def dot(left, right, dims):
    return lax.dot_general(left, right, dims, preferred_element_type=F32)


def halves(value):
    high = value.astype(BF16)
    return high, (value - high.astype(F32)).astype(BF16)


def dot_wide(left, right):
    return dot(
        jnp.concatenate([left, left], axis=1), jnp.concatenate(halves(right), axis=0), NN
    )


def rising(rate, count, first):
    step = lax.broadcasted_iota(jnp.int32, (8, DH), 0).astype(F32) + first
    table, size = jnp.exp(-rate * step), 8
    while size < count:
        table = jnp.concatenate([table, table * jnp.exp(-rate * size)], axis=0)
        size *= 2
    return table


def falling(rate, count, last):
    step = 7.0 + last - lax.broadcasted_iota(jnp.int32, (8, DH), 0).astype(F32)
    table, size = jnp.exp(-rate * step), 8
    while size < count:
        table = jnp.concatenate([table * jnp.exp(-rate * size), table], axis=0)
        size *= 2
    return table


def band(rate, count):
    row = lax.broadcasted_iota(jnp.int32, (TILE, count), 0) + (count - TILE)
    diff = (row - lax.broadcasted_iota(jnp.int32, (TILE, count), 1)).astype(F32)
    wide = jnp.concatenate([rate] * (count // DH), axis=1)
    return jnp.where(diff >= 0, jnp.exp(-wide * jnp.maximum(diff, 0.0)), 0.0)


def fetch(pairs, sems):
    copies = [
        pltpu.make_async_copy(far, near, sems.at[i]) for i, (far, near) in enumerate(pairs)
    ]
    for copy in copies:
        copy.start()
    return copies


def wait(copies):
    for copy in copies:
        copy.wait()


def head(h):
    return slice(h * DH, (h + 1) * DH)


def diagonal():
    return lax.broadcasted_iota(jnp.int32, (TILE, TILE), 0) == lax.broadcasted_iota(
        jnp.int32, (TILE, TILE), 1
    )


def to_rows(part):
    sums = jnp.sum(part, axis=1, keepdims=True)
    mask = diagonal()
    return [
        jnp.sum(jnp.where(mask, sums[a * TILE : (a + 1) * TILE, :], 0.0), axis=0, keepdims=True)
        for a in range(part.shape[0] // TILE)
    ]


def to_columns(table, first, tiles):
    mask = diagonal()
    return jnp.concatenate(
        [
            jnp.sum(jnp.where(mask, table[a : a + 1, :], 0.0), axis=1, keepdims=True)
            for a in range(first, first + tiles)
        ],
        axis=0,
    )


def state_kernel(rate_hbm, k_hbm, v_hbm, out_ref, rate_ref, k_ref, v_ref, sems):
    count, width = k_ref.shape
    copies = fetch(((rate_hbm, rate_ref), (v_hbm, v_ref), (k_hbm, k_ref)), sems)
    copies[0].wait()
    weights = [
        falling(jnp.full((1, DH), rate_ref[h], F32), count, 0.0) for h in range(width // DH)
    ]
    copies[1].wait()
    parts = [
        jnp.concatenate(halves(v_ref[:, head(h)].astype(F32) * weights[h]), axis=1)
        for h in range(width // DH)
    ]
    copies[2].wait()
    for h in range(width // DH):
        sums = dot(k_ref[:, head(h)], parts[h], TN)
        out_ref[head(h), :] = sums[:, :DH] + sums[:, DH:]


def scan_kernel(reverse, decay_ref, in_ref, out_ref):
    blocks = in_ref.shape[0]
    decay = decay_ref[...]
    total = jnp.zeros(in_ref.shape[1:], F32)
    order = range(blocks - 1, -1, -1) if reverse else range(blocks)
    for b in order:
        out_ref[b] = total
        total = total * decay + in_ref[b]


def inner_kernel(
    aux_ref, q_hbm, k_hbm, v_hbm, out_ref, turned_ref, q_ref, k_ref, v_ref, sems
):
    count, width = k_ref.shape
    wait(fetch(((q_hbm, q_ref), (k_hbm, k_ref), (v_hbm, v_ref)), sems))
    for h in range(width // DH):
        table = band(aux_ref[1:2, head(h)], count)
        turned_ref[head(h), :] = q_ref[:, head(h)].T
        for a in range(count // TILE):
            here = slice(a * TILE, (a + 1) * TILE)
            seen = (a + 1) * TILE
            scores = dot(q_ref[here, head(h)], k_ref[:seen, head(h)], NT)
            weights = (scores * table[:, count - seen :]).astype(BF16)
            out_ref[here, head(h)] = dot(weights, v_ref[:seen, head(h)], NN)


def attend_kernel(aux_ref, q_ref, g_ref, inner_ref, prefix_ref, att_ref, sums_ref):
    count, width = q_ref.shape
    squares = jnp.zeros((count, DH), F32)
    crossing = jnp.zeros((count, DH), F32)
    for h in range(width // DH):
        rate = aux_ref[1:2, head(h)]
        weight = rising(rate, count, 1.0)
        attended = (
            inner_ref[:, head(h)] + dot_wide(q_ref[:, head(h)], prefix_ref[head(h), :]) * weight
        )
        att_ref[:, head(h)] = attended
        squares += attended * attended
        crossing += g_ref[:, head(h)].astype(F32) * aux_ref[0:1, head(h)] * attended
    both = jnp.concatenate(to_rows(squares) + to_rows(crossing), axis=0)
    for j in range(sums_ref.shape[0]):
        sums_ref[j] = both


def norm_scales(total, sums_ref):
    tiles = sums_ref.shape[1] // 2
    table = jnp.sum(sums_ref[...], axis=0) / total
    rinv = lax.rsqrt(table[:tiles, :] + 1e-06)
    factor = rinv * rinv * rinv * table[tiles:, :]
    return rinv, factor, tiles


def norm_kernel(
    total, aux_ref, turned_ref, g_ref, att_ref, sums_ref, grad_ref, state_ref
):
    count, width = g_ref.shape
    rinv, factor, tiles = norm_scales(total, sums_ref)
    rinv, factor = to_columns(rinv, 0, tiles), to_columns(factor, 0, tiles)
    for h in range(width // DH):
        scaled = g_ref[:, head(h)].astype(F32) * aux_ref[0:1, head(h)]
        grad = (rinv * scaled - att_ref[:, head(h)] * factor).astype(BF16)
        grad_ref[:, head(h)] = grad
        weight = rising(aux_ref[1:2, head(h)], count, 0.0)
        both = jnp.concatenate(halves(grad.astype(F32) * weight), axis=1)
        sums = dot(turned_ref[head(h), :], both, NN)
        state_ref[head(h), :] = sums[:, :DH] + sums[:, DH:]


def query_kernel(
    total, aux_ref, k_hbm, v_hbm, d_ref, prefix_ref, att_ref, sums_ref,
    normed_ref, dq_ref, k_ref, v_ref, sems,
):
    count, width = k_ref.shape
    copies = fetch(((k_hbm, k_ref), (v_hbm, v_ref)), sems)
    rinv, _, tiles = norm_scales(total, sums_ref)
    rinv = to_columns(rinv, 0, tiles)
    for h in range(width // DH):
        normed_ref[:, head(h)] = (att_ref[:, head(h)] * rinv * aux_ref[0:1, head(h)]).astype(BF16)
    wait(copies)
    for h in range(width // DH):
        rate = aux_ref[1:2, head(h)]
        table = band(rate, count)
        weight = rising(rate, count, 1.0)
        past = dot_wide(d_ref[:, head(h)], prefix_ref[head(h), :].T) * weight
        for a in range(count // TILE):
            here = slice(a * TILE, (a + 1) * TILE)
            seen = (a + 1) * TILE
            scores = dot(d_ref[here, head(h)], v_ref[:seen, head(h)], NT)
            grads = (scores * table[:, count - seen :]).astype(BF16)
            dq_ref[here, head(h)] = (
                dot(grads, k_ref[:seen, head(h)], NN) + past[here, :]
            ).astype(BF16)


def back_kernel(aux_ref, q_hbm, k_hbm, v_hbm, d_ref, dk_ref, dv_ref, q_ref, k_ref, v_ref, sems):
    count, width = q_ref.shape
    wait(fetch(((q_hbm, q_ref), (k_hbm, k_ref), (v_hbm, v_ref)), sems))
    for h in range(width // DH):
        table = band(aux_ref[1:2, head(h)], count)
        for a in range(count // TILE):
            here = slice(a * TILE, (a + 1) * TILE)
            seen = (a + 1) * TILE
            part = table[:, count - seen :]
            q, d = q_ref[here, head(h)], d_ref[here, head(h)]
            weights = (dot(q, k_ref[:seen, head(h)], NT) * part).astype(BF16)
            grads = (dot(d, v_ref[:seen, head(h)], NT) * part).astype(BF16)
            dk, dv = dot(grads, q, TN), dot(weights, d, TN)
            if a:
                before = slice(0, a * TILE)
                dk_ref[before, head(h)] += dk[before, :]
                dv_ref[before, head(h)] += dv[before, :]
            dk_ref[here, head(h)] = dk[here, :]
            dv_ref[here, head(h)] = dv[here, :]


def final_kernel(
    aux_ref, k_ref, v_ref, suffix_ref, dk_ref, dv_ref, kout_hbm, vout_hbm, kout_ref, vout_ref, sems
):
    count, width = k_ref.shape
    copies = []
    for h in range(width // DH):
        tail = falling(aux_ref[1:2, head(h)], count, 1.0)
        suffix = suffix_ref[head(h), :]
        kout_ref[:, head(h)] = (
            dk_ref[:, head(h)] + dot_wide(v_ref[:, head(h)], suffix.T) * tail
        ).astype(BF16)
        vout_ref[:, head(h)] = (
            dv_ref[:, head(h)] + dot_wide(k_ref[:, head(h)], suffix) * tail
        ).astype(BF16)
        for index, (held, out) in enumerate(((kout_ref, kout_hbm), (vout_ref, vout_hbm))):
            copy = pltpu.make_async_copy(
                held.at[:, head(h)], out.at[:, head(h)], sems.at[2 * h + index]
            )
            copy.start()
            copies.append(copy)
    wait(copies)


def call(kernel, shapes, specs, *args, name, flops, size, mib=8, out_specs=None, scratch=()):
    return pl.pallas_call(
        kernel,
        out_shape=shapes,
        in_specs=specs,
        out_specs=out_specs or tuple(VMEM for _ in shapes),
        scratch_shapes=scratch,
        compiler_params=pltpu.CompilerParams(vmem_limit_bytes=mib * 2**20),
        cost_estimate=pl.CostEstimate(flops=flops, bytes_accessed=size, transcendentals=0),
        name=name,
    )(*args)


def scan(state, decay, reverse):
    axes = ("y", "x")
    blocks = lax.axis_size(axes)
    pieces = state.reshape(blocks, -1, DH)
    mine = lax.all_to_all(pieces, axes, 0, 0, tiled=True)
    (sums,) = call(
        functools.partial(scan_kernel, reverse),
        (jax.ShapeDtypeStruct(mine.shape, F32),),
        [VMEM, VMEM],
        decay, mine,
        name="scan", flops=2 * mine.size, size=2 * mine.size * 4, mib=2,
    )
    return lax.all_to_all(sums, axes, 0, 0, tiled=True).reshape(state.shape)


def local(queries, keys, values, out_grad, decay_rate, gain):
    count, width = queries.shape
    heads = decay_rate.shape[0]
    ctx, head_axes = ("y", "x"), ("z", "c")
    shape = jax.ShapeDtypeStruct
    whole, state_shape = (count, width), (width, DH)
    aux = jnp.stack([gain, jnp.repeat(decay_rate, DH)])
    owner = lax.axis_index(ctx) * heads // lax.axis_size(ctx)
    decay = jnp.exp(-lax.dynamic_slice(decay_rate, (owner,), (1,)) * count)
    decay = jnp.broadcast_to(decay[None, :], (1, DH))
    pair = 2 * count * count * DH * heads
    wide = 4 * count * DH * DH * heads
    unit = count * width
    far_rate, far_q, far_k, far_v = (
        pltpu.with_memory_space_constraint(array, pltpu.HBM)
        for array in (decay_rate, queries, keys, values)
    )
    block = pltpu.VMEM(whole, BF16)
    (state,) = call(
        state_kernel, (shape(state_shape, F32),), [ANY] * 3, far_rate, far_k, far_v,
        name="state", flops=wide, size=4 * unit,
        scratch=[pltpu.SMEM((heads,), F32), block, block, pltpu.SemaphoreType.DMA((3,))],
    )
    inner, turned = call(
        inner_kernel, (shape(whole, F32), shape((width, count), BF16)), [VMEM] + [ANY] * 3,
        aux, far_q, far_k, far_v,
        name="inner", flops=2 * pair, size=10 * unit,
        scratch=[block, block, block, pltpu.SemaphoreType.DMA((3,))],
    )
    decay, inner, turned = lax.optimization_barrier((decay, inner, turned))
    prefix = scan(state, decay, False)
    groups = lax.axis_size(head_axes)
    attended, sums = call(
        attend_kernel,
        (shape(whole, F32), shape((groups, 2 * count // TILE, TILE), F32)), [VMEM] * 5,
        aux, queries, out_grad, inner, prefix,
        name="attend", flops=wide, size=12 * unit,
    )
    sums = lax.all_to_all(sums, head_axes, 0, 0, tiled=True)
    total = float(heads * groups * DH)
    grad, state = call(
        functools.partial(norm_kernel, total),
        (shape(whole, BF16), shape(state_shape, F32)), [VMEM] * 5,
        aux, turned, out_grad, attended, sums,
        name="norm", flops=wide, size=12 * unit,
    )
    normed, dq = call(
        functools.partial(query_kernel, total),
        (shape(whole, BF16), shape(whole, BF16)), [VMEM] + [ANY] * 2 + [VMEM] * 4,
        aux, far_k, far_v, grad, prefix, attended, sums,
        name="query", flops=2 * pair, size=16 * unit,
        scratch=[block, block, pltpu.SemaphoreType.DMA((2,))],
    )
    suffix = scan(state, decay, True)
    dk, dv = call(
        back_kernel, (shape(whole, F32), shape(whole, F32)), [VMEM] + [ANY] * 3 + [VMEM],
        aux, far_q, far_k, far_v, grad,
        name="back", flops=4 * pair, size=16 * unit,
        scratch=[block, block, block, pltpu.SemaphoreType.DMA((3,))],
    )
    dk, dv = call(
        final_kernel, (shape(whole, BF16), shape(whole, BF16)), [VMEM] * 6,
        aux, keys, values, suffix, dk, dv,
        name="final", flops=2 * wide, size=20 * unit, out_specs=(ANY, ANY),
        scratch=[block, block, pltpu.SemaphoreType.DMA((2 * heads,))],
    )
    return normed, dq, dk, dv


def solution(mesh):
    fine = Mesh(mesh.devices.reshape(8, 4, 8, 2), ("y", "x", "z", "c"))
    ctx, head_axes = ("y", "x"), ("z", "c")
    tokens = P(ctx, head_axes)
    return jax.shard_map(
        local,
        mesh=fine,
        in_specs=(tokens,) * 4 + (P(head_axes),) * 2,
        out_specs=(tokens,) * 4,
        check_vma=False,
    )
```

```python
import functools

import jax
import jax.numpy as jnp
from jax import lax
from jax.experimental import pallas as pl
from jax.experimental.pallas import tpu as pltpu
from jax.sharding import PartitionSpec as P

DH = 128
TILE = 128
FIRST_CTX = 18
FIRST_HEAD = 11
F32 = jnp.float32
BF16 = jnp.bfloat16
NT = (((1,), (1,)), ((), ()))
TN = (((0,), (0,)), ((), ()))
NN = (((1,), (0,)), ((), ()))
VMEM = pl.BlockSpec(memory_space=pltpu.VMEM)
SMEM = pl.BlockSpec(memory_space=pltpu.SMEM)
ANY = pl.BlockSpec(memory_space=pl.ANY)


def dot(left, right, dims):
    return lax.dot_general(left, right, dims, preferred_element_type=F32)


def halves(value):
    high = value.astype(BF16)
    return high, (value - high.astype(F32)).astype(BF16)


def dot_wide(left, right):
    return dot(
        jnp.concatenate([left, left], axis=1), jnp.concatenate(halves(right), axis=0), NN
    )


def rising(rate, count, first):
    step = lax.broadcasted_iota(jnp.int32, (8, DH), 0).astype(F32) + first
    table, size = jnp.exp(-rate * step), 8
    while size < count:
        table = jnp.concatenate([table, table * jnp.exp(-rate * size)], axis=0)
        size *= 2
    return table


def falling(rate, count, last):
    step = 7.0 + last - lax.broadcasted_iota(jnp.int32, (8, DH), 0).astype(F32)
    table, size = jnp.exp(-rate * step), 8
    while size < count:
        table = jnp.concatenate([table * jnp.exp(-rate * size), table], axis=0)
        size *= 2
    return table


def band(rate, count):
    row = lax.broadcasted_iota(jnp.int32, (TILE, count), 0) + (count - TILE)
    diff = (row - lax.broadcasted_iota(jnp.int32, (TILE, count), 1)).astype(F32)
    wide = jnp.concatenate([rate] * (count // DH), axis=1)
    return jnp.where(diff >= 0, jnp.exp(-wide * jnp.maximum(diff, 0.0)), 0.0)


def fetch(pairs, sems):
    copies = [
        pltpu.make_async_copy(far, near, sems.at[i]) for i, (far, near) in enumerate(pairs)
    ]
    for copy in copies:
        copy.start()
    return copies


def wait(copies):
    for copy in copies:
        copy.wait()


def head(h):
    return slice(h * DH, (h + 1) * DH)


def diagonal():
    return lax.broadcasted_iota(jnp.int32, (TILE, TILE), 0) == lax.broadcasted_iota(
        jnp.int32, (TILE, TILE), 1
    )


def to_rows(part):
    sums = jnp.sum(part, axis=1, keepdims=True)
    mask = diagonal()
    return [
        jnp.sum(jnp.where(mask, sums[a * TILE : (a + 1) * TILE, :], 0.0), axis=0, keepdims=True)
        for a in range(part.shape[0] // TILE)
    ]


def to_columns(table, first, tiles):
    mask = diagonal()
    return jnp.concatenate(
        [
            jnp.sum(jnp.where(mask, table[a : a + 1, :], 0.0), axis=1, keepdims=True)
            for a in range(first, first + tiles)
        ],
        axis=0,
    )


def state_kernel(rate_hbm, k_hbm, v_hbm, out_ref, rows_ref, rate_ref, k_ref, v_ref, sems):
    count, width = k_ref.shape
    copies = fetch(((rate_hbm, rate_ref), (v_hbm, v_ref), (k_hbm, k_ref)), sems)
    copies[0].wait()
    weights = [
        falling(jnp.full((1, DH), rate_ref[h], F32), count, 0.0) for h in range(width // DH)
    ]
    for h in range(width // DH):
        rate = jnp.full((1, DH), rate_ref[h], F32)
        rows_ref[1:2, head(h)] = rate
        rows_ref[2:3, head(h)] = jnp.exp(-rate * count)
    copies[1].wait()
    parts = [
        jnp.concatenate(halves(v_ref[:, head(h)].astype(F32) * weights[h]), axis=1)
        for h in range(width // DH)
    ]
    copies[2].wait()
    for h in range(width // DH):
        sums = dot(k_ref[:, head(h)], parts[h], TN)
        out_ref[head(h), :] = sums[:, :DH] + sums[:, DH:]


def scan_kernel(reverse, first, heads, aux_ref, in_ref, out_ref):
    blocks = in_ref.shape[0]
    place = lax.rem(lax.axis_index("ctx") + (blocks - first), blocks)
    owner = lax.div(place * heads, blocks)
    decay = aux_ref[2:3, pl.ds(pl.multiple_of(owner * DH, DH), DH)]
    total = jnp.zeros(in_ref.shape[1:], F32)
    order = range(blocks - 1, -1, -1) if reverse else range(blocks)
    for b in order:
        place = (b - first) % blocks
        out_ref[place] = total
        total = total * decay + in_ref[place]


def inner_kernel(
    rows_ref, gain_ref, q_hbm, k_hbm, v_hbm, out_ref, aux_ref, q_ref, k_ref, v_ref, sems
):
    count, width = k_ref.shape
    aux_ref[...] = rows_ref[...]
    aux_ref[0:1, :] = gain_ref[...]
    wait(fetch(((q_hbm, q_ref), (k_hbm, k_ref), (v_hbm, v_ref)), sems))
    for h in range(width // DH):
        table = band(rows_ref[1:2, head(h)], count)
        for a in range(count // TILE):
            here = slice(a * TILE, (a + 1) * TILE)
            seen = (a + 1) * TILE
            scores = dot(q_ref[here, head(h)], k_ref[:seen, head(h)], NT)
            weights = (scores * table[:, count - seen :]).astype(BF16)
            out_ref[here, head(h)] = dot(weights, v_ref[:seen, head(h)], NN)


def attend_kernel(aux_ref, q_ref, g_ref, inner_ref, prefix_ref, att_ref, sums_ref):
    count, width = q_ref.shape
    squares = jnp.zeros((count, DH), F32)
    crossing = jnp.zeros((count, DH), F32)
    for h in range(width // DH):
        rate = aux_ref[1:2, head(h)]
        weight = rising(rate, count, 1.0)
        attended = (
            inner_ref[:, head(h)] + dot_wide(q_ref[:, head(h)], prefix_ref[head(h), :]) * weight
        )
        att_ref[:, head(h)] = attended
        squares += attended * attended
        crossing += g_ref[:, head(h)].astype(F32) * aux_ref[0:1, head(h)] * attended
    both = jnp.concatenate(to_rows(squares) + to_rows(crossing), axis=0)
    for j in range(sums_ref.shape[0]):
        sums_ref[j] = both


def norm_scales(total, sums_ref):
    tiles = sums_ref.shape[1] // 2
    table = jnp.sum(sums_ref[...], axis=0) / total
    rinv = lax.rsqrt(table[:tiles, :] + 1e-06)
    factor = rinv * rinv * rinv * table[tiles:, :]
    return rinv, factor, tiles


def norm_kernel(
    total, aux_ref, q_ref, g_ref, att_ref, sums_ref, grad_ref, state_ref
):
    count, width = g_ref.shape
    rinv, factor, tiles = norm_scales(total, sums_ref)
    rinv, factor = to_columns(rinv, 0, tiles), to_columns(factor, 0, tiles)
    for h in range(width // DH):
        scaled = g_ref[:, head(h)].astype(F32) * aux_ref[0:1, head(h)]
        grad = (rinv * scaled - att_ref[:, head(h)] * factor).astype(BF16)
        grad_ref[:, head(h)] = grad
        weight = rising(aux_ref[1:2, head(h)], count, 0.0)
        both = jnp.concatenate(halves(grad.astype(F32) * weight), axis=1)
        sums = dot(q_ref[:, head(h)], both, TN)
        state_ref[head(h), :] = sums[:, :DH] + sums[:, DH:]


def query_kernel(
    total, aux_ref, k_hbm, v_hbm, d_ref, prefix_ref, att_ref, sums_ref,
    normed_ref, dq_ref, k_ref, v_ref, sems,
):
    count, width = k_ref.shape
    copies = fetch(((k_hbm, k_ref), (v_hbm, v_ref)), sems)
    rinv, _, tiles = norm_scales(total, sums_ref)
    rinv = to_columns(rinv, 0, tiles)
    for h in range(width // DH):
        normed_ref[:, head(h)] = (att_ref[:, head(h)] * rinv * aux_ref[0:1, head(h)]).astype(BF16)
    wait(copies)
    for h in range(width // DH):
        rate = aux_ref[1:2, head(h)]
        table = band(rate, count)
        weight = rising(rate, count, 1.0)
        past = dot_wide(d_ref[:, head(h)], prefix_ref[head(h), :].T) * weight
        for a in range(count // TILE):
            here = slice(a * TILE, (a + 1) * TILE)
            seen = (a + 1) * TILE
            scores = dot(d_ref[here, head(h)], v_ref[:seen, head(h)], NT)
            grads = (scores * table[:, count - seen :]).astype(BF16)
            dq_ref[here, head(h)] = (
                dot(grads, k_ref[:seen, head(h)], NN) + past[here, :]
            ).astype(BF16)


def back_kernel(aux_ref, q_hbm, k_hbm, v_hbm, d_ref, dk_ref, dv_ref, q_ref, k_ref, v_ref, sems):
    count, width = q_ref.shape
    wait(fetch(((q_hbm, q_ref), (k_hbm, k_ref), (v_hbm, v_ref)), sems))
    for h in range(width // DH):
        table = band(aux_ref[1:2, head(h)], count)
        for a in range(count // TILE):
            here = slice(a * TILE, (a + 1) * TILE)
            seen = (a + 1) * TILE
            part = table[:, count - seen :]
            q, d = q_ref[here, head(h)], d_ref[here, head(h)]
            weights = (dot(q, k_ref[:seen, head(h)], NT) * part).astype(BF16)
            grads = (dot(d, v_ref[:seen, head(h)], NT) * part).astype(BF16)
            dk, dv = dot(grads, q, TN), dot(weights, d, TN)
            if a:
                before = slice(0, a * TILE)
                dk_ref[before, head(h)] += dk[before, :]
                dv_ref[before, head(h)] += dv[before, :]
            dk_ref[here, head(h)] = dk[here, :]
            dv_ref[here, head(h)] = dv[here, :]


def final_kernel(
    aux_ref, k_ref, v_ref, suffix_ref, dk_ref, dv_ref, kout_hbm, vout_hbm, kout_ref, vout_ref, sems
):
    count, width = k_ref.shape
    copies = []
    for h in range(width // DH):
        tail = falling(aux_ref[1:2, head(h)], count, 1.0)
        suffix = suffix_ref[head(h), :]
        kout_ref[:, head(h)] = (
            dk_ref[:, head(h)] + dot_wide(v_ref[:, head(h)], suffix.T) * tail
        ).astype(BF16)
        vout_ref[:, head(h)] = (
            dv_ref[:, head(h)] + dot_wide(k_ref[:, head(h)], suffix) * tail
        ).astype(BF16)
        for index, (held, out) in enumerate(((kout_ref, kout_hbm), (vout_ref, vout_hbm))):
            copy = pltpu.make_async_copy(
                held.at[:, head(h)], out.at[:, head(h)], sems.at[2 * h + index]
            )
            copy.start()
            copies.append(copy)
    wait(copies)


def call(kernel, shapes, specs, *args, name, flops, size, mib=8, out_specs=None, scratch=()):
    return pl.pallas_call(
        kernel,
        out_shape=shapes,
        in_specs=specs,
        out_specs=out_specs or tuple(VMEM for _ in shapes),
        scratch_shapes=scratch,
        compiler_params=pltpu.CompilerParams(vmem_limit_bytes=mib * 2**20),
        cost_estimate=pl.CostEstimate(flops=flops, bytes_accessed=size, transcendentals=0),
        name=name,
    )(*args)


def exchange(pieces, axis, first):
    size = lax.axis_size(axis)
    order = [(first + j) % size for j in range(size)]
    return lax.all_to_all(pieces, axis, 0, 0, tiled=True, axis_index_groups=[order])


def scan(state, aux, heads, first, reverse):
    pieces = state.reshape(lax.axis_size("ctx"), -1, DH)
    mine = exchange(pieces, "ctx", first)
    (sums,) = call(
        functools.partial(scan_kernel, reverse, first, heads),
        (jax.ShapeDtypeStruct(mine.shape, F32),),
        [VMEM, VMEM],
        aux, mine,
        name="scan", flops=2 * mine.size, size=2 * mine.size * 4, mib=2,
    )
    return exchange(sums, "ctx", first).reshape(state.shape)


def local(queries, keys, values, out_grad, decay_rate, gain):
    count, width = queries.shape
    heads = decay_rate.shape[0]
    shape = jax.ShapeDtypeStruct
    whole, state_shape = (count, width), (width, DH)
    groups = lax.axis_size("head")
    middle, late = FIRST_CTX, FIRST_HEAD
    pair = 2 * count * count * DH * heads
    wide = 4 * count * DH * DH * heads
    unit = count * width
    far_rate, far_q, far_k, far_v = (
        pltpu.with_memory_space_constraint(array, pltpu.HBM)
        for array in (decay_rate, queries, keys, values)
    )
    block = pltpu.VMEM(whole, BF16)
    state, rows = call(
        state_kernel, (shape(state_shape, F32), shape((8, width), F32)), [ANY] * 3, far_rate, far_k, far_v,
        name="state", flops=wide, size=4 * unit,
        scratch=[pltpu.SMEM((heads,), F32), block, block, pltpu.SemaphoreType.DMA((3,))],
    )
    inner, aux = call(
        inner_kernel, (shape(whole, F32), shape((8, width), F32)), [VMEM] * 2 + [ANY] * 3,
        rows, gain[None, :], far_q, far_k, far_v,
        name="inner", flops=2 * pair, size=10 * unit,
        scratch=[block, block, block, pltpu.SemaphoreType.DMA((3,))],
    )
    prefix = scan(state, aux, heads, middle, False)
    attended, sums = call(
        attend_kernel,
        (shape(whole, F32), shape((groups, 2 * count // TILE, TILE), F32)), [VMEM] * 5,
        aux, queries, out_grad, inner, prefix,
        name="attend", flops=wide, size=12 * unit,
    )
    sums = exchange(sums, "head", late)
    total = float(heads * groups * DH)
    grad, state = call(
        functools.partial(norm_kernel, total),
        (shape(whole, BF16), shape(state_shape, F32)), [VMEM] * 5,
        aux, queries, out_grad, attended, sums,
        name="norm", flops=wide, size=12 * unit,
    )
    normed, dq = call(
        functools.partial(query_kernel, total),
        (shape(whole, BF16), shape(whole, BF16)), [VMEM] + [ANY] * 2 + [VMEM] * 4,
        aux, far_k, far_v, grad, prefix, attended, sums,
        name="query", flops=2 * pair, size=16 * unit,
        scratch=[block, block, pltpu.SemaphoreType.DMA((2,))],
    )
    aux, normed, dq = lax.optimization_barrier((aux, normed, dq))
    suffix = scan(state, aux, heads, middle, True)
    dk, dv = call(
        back_kernel, (shape(whole, F32), shape(whole, F32)), [VMEM] + [ANY] * 3 + [VMEM],
        aux, far_q, far_k, far_v, grad,
        name="back", flops=4 * pair, size=16 * unit,
        scratch=[block, block, block, pltpu.SemaphoreType.DMA((3,))],
    )
    dk, dv = call(
        final_kernel, (shape(whole, BF16), shape(whole, BF16)), [VMEM] * 6,
        aux, keys, values, suffix, dk, dv,
        name="final", flops=2 * wide, size=20 * unit, out_specs=(ANY, ANY),
        scratch=[block, block, pltpu.SemaphoreType.DMA((2 * heads,))],
    )
    return normed, dq, dk, dv


def solution(mesh):
    tokens = P("ctx", "head")
    return jax.shard_map(
        local,
        mesh=mesh,
        in_specs=(tokens,) * 4 + (P("head"),) * 2,
        out_specs=(tokens,) * 4,
        check_vma=False,
    )
```

```python
import functools

import jax
import jax.numpy as jnp
from jax import lax
from jax.experimental import pallas as pl
from jax.experimental.pallas import tpu as pltpu
from jax.sharding import PartitionSpec as P

DH = 128
TILE = 128
FIRST_CTX = 18
FIRST_HEAD = 11
F32 = jnp.float32
BF16 = jnp.bfloat16
NT = (((1,), (1,)), ((), ()))
TN = (((0,), (0,)), ((), ()))
NN = (((1,), (0,)), ((), ()))
VMEM = pl.BlockSpec(memory_space=pltpu.VMEM)
SMEM = pl.BlockSpec(memory_space=pltpu.SMEM)
ANY = pl.BlockSpec(memory_space=pl.ANY)


def dot(left, right, dims):
    return lax.dot_general(left, right, dims, preferred_element_type=F32)


def halves(value):
    high = value.astype(BF16)
    return high, (value - high.astype(F32)).astype(BF16)


def dot_wide(left, right):
    return dot(
        jnp.concatenate([left, left], axis=1), jnp.concatenate(halves(right), axis=0), NN
    )


def rising(rate, count, first):
    step = lax.broadcasted_iota(jnp.int32, (8, DH), 0).astype(F32) + first
    table, size = jnp.exp(-rate * step), 8
    while size < count:
        table = jnp.concatenate([table, table * jnp.exp(-rate * size)], axis=0)
        size *= 2
    return table


def falling(rate, count, last):
    step = 7.0 + last - lax.broadcasted_iota(jnp.int32, (8, DH), 0).astype(F32)
    table, size = jnp.exp(-rate * step), 8
    while size < count:
        table = jnp.concatenate([table * jnp.exp(-rate * size), table], axis=0)
        size *= 2
    return table


def band(rate, count):
    row = lax.broadcasted_iota(jnp.int32, (TILE, count), 0) + (count - TILE)
    diff = (row - lax.broadcasted_iota(jnp.int32, (TILE, count), 1)).astype(F32)
    wide = jnp.concatenate([rate] * (count // DH), axis=1)
    return jnp.where(diff >= 0, jnp.exp(-wide * jnp.maximum(diff, 0.0)), 0.0)


def fetch(pairs, sems):
    copies = [
        pltpu.make_async_copy(far, near, sems.at[i]) for i, (far, near) in enumerate(pairs)
    ]
    for copy in copies:
        copy.start()
    return copies


def wait(copies):
    for copy in copies:
        copy.wait()


def head(h):
    return slice(h * DH, (h + 1) * DH)


def diagonal():
    return lax.broadcasted_iota(jnp.int32, (TILE, TILE), 0) == lax.broadcasted_iota(
        jnp.int32, (TILE, TILE), 1
    )


def to_rows(part):
    sums = jnp.sum(part, axis=1, keepdims=True)
    mask = diagonal()
    return [
        jnp.sum(jnp.where(mask, sums[a * TILE : (a + 1) * TILE, :], 0.0), axis=0, keepdims=True)
        for a in range(part.shape[0] // TILE)
    ]


def to_columns(table, first, tiles):
    mask = diagonal()
    return jnp.concatenate(
        [
            jnp.sum(jnp.where(mask, table[a : a + 1, :], 0.0), axis=1, keepdims=True)
            for a in range(first, first + tiles)
        ],
        axis=0,
    )


def state_kernel(rate_hbm, k_hbm, v_hbm, out_ref, rows_ref, rate_ref, k_ref, v_ref, sems):
    count, width = k_ref.shape
    copies = fetch(((rate_hbm, rate_ref), (v_hbm, v_ref), (k_hbm, k_ref)), sems)
    copies[0].wait()
    weights = [
        falling(jnp.full((1, DH), rate_ref[h], F32), count, 0.0) for h in range(width // DH)
    ]
    for h in range(width // DH):
        rate = jnp.full((1, DH), rate_ref[h], F32)
        rows_ref[1:2, head(h)] = rate
        rows_ref[2:3, head(h)] = jnp.exp(-rate * count)
    copies[1].wait()
    parts = [
        jnp.concatenate(halves(v_ref[:, head(h)].astype(F32) * weights[h]), axis=1)
        for h in range(width // DH)
    ]
    copies[2].wait()
    for h in range(width // DH):
        sums = dot(k_ref[:, head(h)], parts[h], TN)
        out_ref[head(h), :] = sums[:, :DH] + sums[:, DH:]


def scan_kernel(reverse, first, heads, aux_ref, in_ref, out_ref):
    blocks = in_ref.shape[0]
    place = lax.rem(lax.axis_index("ctx") + (blocks - first), blocks)
    owner = lax.div(place * heads, blocks)
    decay = aux_ref[2:3, pl.ds(pl.multiple_of(owner * DH, DH), DH)]
    total = jnp.zeros(in_ref.shape[1:], F32)
    order = range(blocks - 1, -1, -1) if reverse else range(blocks)
    for b in order:
        place = (b - first) % blocks
        out_ref[place] = total
        total = total * decay + in_ref[place]


def inner_kernel(
    rows_ref, gain_ref, q_hbm, k_hbm, v_hbm, out_ref, aux_ref, q_ref, k_ref, v_ref, sems
):
    count, width = k_ref.shape
    aux_ref[...] = rows_ref[...]
    aux_ref[0:1, :] = gain_ref[...]
    wait(fetch(((q_hbm, q_ref), (k_hbm, k_ref), (v_hbm, v_ref)), sems))
    for h in range(width // DH):
        table = band(rows_ref[1:2, head(h)], count)
        for a in range(count // TILE):
            here = slice(a * TILE, (a + 1) * TILE)
            seen = (a + 1) * TILE
            scores = dot(q_ref[here, head(h)], k_ref[:seen, head(h)], NT)
            weights = (scores * table[:, count - seen :]).astype(BF16)
            out_ref[here, head(h)] = dot(weights, v_ref[:seen, head(h)], NN)


def attend_kernel(aux_ref, q_ref, g_ref, inner_ref, prefix_ref, att_ref, sums_ref):
    count, width = q_ref.shape
    squares = jnp.zeros((count, DH), F32)
    crossing = jnp.zeros((count, DH), F32)
    for h in range(width // DH):
        rate = aux_ref[1:2, head(h)]
        weight = rising(rate, count, 1.0)
        attended = (
            inner_ref[:, head(h)] + dot_wide(q_ref[:, head(h)], prefix_ref[head(h), :]) * weight
        )
        att_ref[:, head(h)] = attended
        squares += attended * attended
        crossing += g_ref[:, head(h)].astype(F32) * aux_ref[0:1, head(h)] * attended
    both = jnp.concatenate(to_rows(squares) + to_rows(crossing), axis=0)
    for j in range(sums_ref.shape[0]):
        sums_ref[j] = both


def norm_scales(total, sums_ref):
    tiles = sums_ref.shape[1] // 2
    table = jnp.sum(sums_ref[...], axis=0) / total
    rinv = lax.rsqrt(table[:tiles, :] + 1e-06)
    factor = rinv * rinv * rinv * table[tiles:, :]
    return rinv, factor, tiles


def norm_kernel(
    total, aux_ref, q_ref, g_ref, att_ref, sums_ref, grad_ref, state_ref
):
    count, width = g_ref.shape
    rinv, factor, tiles = norm_scales(total, sums_ref)
    rinv, factor = to_columns(rinv, 0, tiles), to_columns(factor, 0, tiles)
    for h in range(width // DH):
        scaled = g_ref[:, head(h)].astype(F32) * aux_ref[0:1, head(h)]
        grad = (rinv * scaled - att_ref[:, head(h)] * factor).astype(BF16)
        grad_ref[:, head(h)] = grad
        weight = rising(aux_ref[1:2, head(h)], count, 0.0)
        both = jnp.concatenate(halves(grad.astype(F32) * weight), axis=1)
        sums = dot(q_ref[:, head(h)], both, TN)
        state_ref[head(h), :] = sums[:, :DH] + sums[:, DH:]


def query_kernel(
    total, aux_ref, k_hbm, v_hbm, d_ref, prefix_ref, att_ref, sums_ref,
    normed_ref, dq_ref, k_ref, v_ref, sems,
):
    count, width = k_ref.shape
    copies = fetch(((k_hbm, k_ref), (v_hbm, v_ref)), sems)
    rinv, _, tiles = norm_scales(total, sums_ref)
    rinv = to_columns(rinv, 0, tiles)
    for h in range(width // DH):
        normed_ref[:, head(h)] = (att_ref[:, head(h)] * rinv * aux_ref[0:1, head(h)]).astype(BF16)
    wait(copies)
    for h in range(width // DH):
        rate = aux_ref[1:2, head(h)]
        table = band(rate, count)
        weight = rising(rate, count, 1.0)
        past = dot_wide(d_ref[:, head(h)], prefix_ref[head(h), :].T) * weight
        for a in range(count // TILE):
            here = slice(a * TILE, (a + 1) * TILE)
            seen = (a + 1) * TILE
            scores = dot(d_ref[here, head(h)], v_ref[:seen, head(h)], NT)
            grads = (scores * table[:, count - seen :]).astype(BF16)
            dq_ref[here, head(h)] = (
                dot(grads, k_ref[:seen, head(h)], NN) + past[here, :]
            ).astype(BF16)


def back_kernel(
    aux_ref, q_hbm, k_hbm, v_hbm, d_hbm, dk_ref, dv_ref, q_ref, k_ref, v_ref, d_ref, sems
):
    count, width = q_ref.shape
    wait(fetch(((q_hbm, q_ref), (k_hbm, k_ref), (v_hbm, v_ref), (d_hbm, d_ref)), sems))
    for h in range(width // DH):
        table = band(aux_ref[1:2, head(h)], count)
        for a in range(count // TILE):
            here = slice(a * TILE, (a + 1) * TILE)
            seen = (a + 1) * TILE
            part = table[:, count - seen :]
            q, d = q_ref[here, head(h)], d_ref[here, head(h)]
            weights = (dot(q, k_ref[:seen, head(h)], NT) * part).astype(BF16)
            grads = (dot(d, v_ref[:seen, head(h)], NT) * part).astype(BF16)
            dk, dv = dot(grads, q, TN), dot(weights, d, TN)
            if a:
                before = slice(0, a * TILE)
                dk_ref[before, head(h)] += dk[before, :]
                dv_ref[before, head(h)] += dv[before, :]
            dk_ref[here, head(h)] = dk[here, :]
            dv_ref[here, head(h)] = dv[here, :]


def final_kernel(
    aux_ref, k_ref, v_ref, suffix_ref, dk_ref, dv_ref, kout_hbm, vout_hbm, kout_ref, vout_ref, sems
):
    count, width = k_ref.shape
    copies = []
    for h in range(width // DH):
        tail = falling(aux_ref[1:2, head(h)], count, 1.0)
        suffix = suffix_ref[head(h), :]
        kout_ref[:, head(h)] = (
            dk_ref[:, head(h)] + dot_wide(v_ref[:, head(h)], suffix.T) * tail
        ).astype(BF16)
        vout_ref[:, head(h)] = (
            dv_ref[:, head(h)] + dot_wide(k_ref[:, head(h)], suffix) * tail
        ).astype(BF16)
        for index, (held, out) in enumerate(((kout_ref, kout_hbm), (vout_ref, vout_hbm))):
            copy = pltpu.make_async_copy(
                held.at[:, head(h)], out.at[:, head(h)], sems.at[2 * h + index]
            )
            copy.start()
            copies.append(copy)
    wait(copies)


def call(kernel, shapes, specs, *args, name, flops, size, mib=8, out_specs=None, scratch=()):
    return pl.pallas_call(
        kernel,
        out_shape=shapes,
        in_specs=specs,
        out_specs=out_specs or tuple(VMEM for _ in shapes),
        scratch_shapes=scratch,
        compiler_params=pltpu.CompilerParams(vmem_limit_bytes=mib * 2**20),
        cost_estimate=pl.CostEstimate(flops=flops, bytes_accessed=size, transcendentals=0),
        name=name,
    )(*args)


def exchange(pieces, axis, first):
    size = lax.axis_size(axis)
    order = [(first + j) % size for j in range(size)]
    return lax.all_to_all(pieces, axis, 0, 0, tiled=True, axis_index_groups=[order])


def scan(state, aux, heads, first, reverse):
    pieces = state.reshape(lax.axis_size("ctx"), -1, DH)
    mine = exchange(pieces, "ctx", first)
    (sums,) = call(
        functools.partial(scan_kernel, reverse, first, heads),
        (jax.ShapeDtypeStruct(mine.shape, F32),),
        [VMEM, VMEM],
        aux, mine,
        name="scan", flops=2 * mine.size, size=2 * mine.size * 4, mib=2,
    )
    return exchange(sums, "ctx", first).reshape(state.shape)


def local(queries, keys, values, out_grad, decay_rate, gain):
    count, width = queries.shape
    heads = decay_rate.shape[0]
    shape = jax.ShapeDtypeStruct
    whole, state_shape = (count, width), (width, DH)
    groups = lax.axis_size("head")
    middle, late = FIRST_CTX, FIRST_HEAD
    pair = 2 * count * count * DH * heads
    wide = 4 * count * DH * DH * heads
    unit = count * width
    far_rate, far_q, far_k, far_v = (
        pltpu.with_memory_space_constraint(array, pltpu.HBM)
        for array in (decay_rate, queries, keys, values)
    )
    block = pltpu.VMEM(whole, BF16)
    state, rows = call(
        state_kernel, (shape(state_shape, F32), shape((8, width), F32)), [ANY] * 3, far_rate, far_k, far_v,
        name="state", flops=wide, size=4 * unit,
        scratch=[pltpu.SMEM((heads,), F32), block, block, pltpu.SemaphoreType.DMA((3,))],
    )
    inner, aux = call(
        inner_kernel, (shape(whole, F32), shape((8, width), F32)), [VMEM] * 2 + [ANY] * 3,
        rows, gain[None, :], far_q, far_k, far_v,
        name="inner", flops=2 * pair, size=10 * unit,
        scratch=[block, block, block, pltpu.SemaphoreType.DMA((3,))],
    )
    prefix = scan(state, aux, heads, middle, False)
    attended, sums = call(
        attend_kernel,
        (shape(whole, F32), shape((groups, 2 * count // TILE, TILE), F32)), [VMEM] * 5,
        aux, queries, out_grad, inner, prefix,
        name="attend", flops=wide, size=12 * unit,
    )
    sums = exchange(sums, "head", late)
    total = float(heads * groups * DH)
    grad, state = call(
        functools.partial(norm_kernel, total),
        (shape(whole, BF16), shape(state_shape, F32)), [VMEM] * 5,
        aux, queries, out_grad, attended, sums,
        name="norm", flops=wide, size=12 * unit,
    )
    normed, dq = call(
        functools.partial(query_kernel, total),
        (shape(whole, BF16), shape(whole, BF16)), [VMEM] + [ANY] * 2 + [VMEM] * 4,
        aux, far_k, far_v, grad, prefix, attended, sums,
        name="query", flops=2 * pair, size=16 * unit,
        scratch=[block, block, pltpu.SemaphoreType.DMA((2,))],
    )
    aux, normed, dq = lax.optimization_barrier((aux, normed, dq))
    suffix = scan(state, aux, heads, middle, True)
    dk, dv = call(
        back_kernel, (shape(whole, F32), shape(whole, F32)), [VMEM] + [ANY] * 4,
        aux, far_q, far_k, far_v, pltpu.with_memory_space_constraint(grad, pltpu.HBM),
        name="back", flops=4 * pair, size=16 * unit,
        scratch=[block, block, block, block, pltpu.SemaphoreType.DMA((4,))],
    )
    dk, dv = call(
        final_kernel, (shape(whole, BF16), shape(whole, BF16)), [VMEM] * 6,
        aux, keys, values, suffix, dk, dv,
        name="final", flops=2 * wide, size=20 * unit, out_specs=(ANY, ANY),
        scratch=[block, block, pltpu.SemaphoreType.DMA((2 * heads,))],
    )
    return normed, dq, dk, dv


def solution(mesh):
    tokens = P("ctx", "head")
    return jax.shard_map(
        local,
        mesh=mesh,
        in_specs=(tokens,) * 4 + (P("head"),) * 2,
        out_specs=(tokens,) * 4,
        check_vma=False,
    )
```

```python
import functools

import jax
import jax.numpy as jnp
from jax import lax
from jax.experimental import pallas as pl
from jax.experimental.pallas import tpu as pltpu
from jax.sharding import PartitionSpec as P

DH = 128
TILE = 128
FIRST_CTX = 18
FIRST_HEAD = 11
F32 = jnp.float32
BF16 = jnp.bfloat16
NT = (((1,), (1,)), ((), ()))
TN = (((0,), (0,)), ((), ()))
NN = (((1,), (0,)), ((), ()))
VMEM = pl.BlockSpec(memory_space=pltpu.VMEM)
SMEM = pl.BlockSpec(memory_space=pltpu.SMEM)
ANY = pl.BlockSpec(memory_space=pl.ANY)


def dot(left, right, dims):
    return lax.dot_general(left, right, dims, preferred_element_type=F32)


def halves(value):
    high = value.astype(BF16)
    return high, (value - high.astype(F32)).astype(BF16)


def dot_wide(left, right):
    return dot(
        jnp.concatenate([left, left], axis=1), jnp.concatenate(halves(right), axis=0), NN
    )


def rising(rate, count, first):
    step = lax.broadcasted_iota(jnp.int32, (8, DH), 0).astype(F32) + first
    table, size = jnp.exp(-rate * step), 8
    while size < count:
        table = jnp.concatenate([table, table * jnp.exp(-rate * size)], axis=0)
        size *= 2
    return table


def falling(rate, count, last):
    step = 7.0 + last - lax.broadcasted_iota(jnp.int32, (8, DH), 0).astype(F32)
    table, size = jnp.exp(-rate * step), 8
    while size < count:
        table = jnp.concatenate([table * jnp.exp(-rate * size), table], axis=0)
        size *= 2
    return table


def band(rate, count):
    row = lax.broadcasted_iota(jnp.int32, (TILE, count), 0) + (count - TILE)
    diff = (row - lax.broadcasted_iota(jnp.int32, (TILE, count), 1)).astype(F32)
    wide = jnp.concatenate([rate] * (count // DH), axis=1)
    return jnp.where(diff >= 0, jnp.exp(-wide * jnp.maximum(diff, 0.0)), 0.0)


def fetch(pairs, sems):
    copies = [
        pltpu.make_async_copy(far, near, sems.at[i]) for i, (far, near) in enumerate(pairs)
    ]
    for copy in copies:
        copy.start()
    return copies


def wait(copies):
    for copy in copies:
        copy.wait()


def head(h):
    return slice(h * DH, (h + 1) * DH)


def diagonal():
    return lax.broadcasted_iota(jnp.int32, (TILE, TILE), 0) == lax.broadcasted_iota(
        jnp.int32, (TILE, TILE), 1
    )


def to_rows(part):
    sums = jnp.sum(part, axis=1, keepdims=True)
    mask = diagonal()
    return [
        jnp.sum(jnp.where(mask, sums[a * TILE : (a + 1) * TILE, :], 0.0), axis=0, keepdims=True)
        for a in range(part.shape[0] // TILE)
    ]


def to_columns(table, first, tiles):
    mask = diagonal()
    return jnp.concatenate(
        [
            jnp.sum(jnp.where(mask, table[a : a + 1, :], 0.0), axis=1, keepdims=True)
            for a in range(first, first + tiles)
        ],
        axis=0,
    )


def state_kernel(rate_hbm, k_hbm, v_hbm, out_ref, rows_ref, rate_ref, k_ref, v_ref, sems):
    count, width = k_ref.shape
    copies = fetch(((rate_hbm, rate_ref), (v_hbm, v_ref), (k_hbm, k_ref)), sems)
    copies[0].wait()
    weights = [
        falling(jnp.full((1, DH), rate_ref[h], F32), count, 0.0) for h in range(width // DH)
    ]
    for h in range(width // DH):
        rate = jnp.full((1, DH), rate_ref[h], F32)
        rows_ref[1:2, head(h)] = rate
        rows_ref[2:3, head(h)] = jnp.exp(-rate * count)
    copies[1].wait()
    parts = [
        jnp.concatenate(halves(v_ref[:, head(h)].astype(F32) * weights[h]), axis=1)
        for h in range(width // DH)
    ]
    copies[2].wait()
    for h in range(width // DH):
        sums = dot(k_ref[:, head(h)], parts[h], TN)
        out_ref[head(h), :] = sums[:, :DH] + sums[:, DH:]


def scan_kernel(reverse, first, heads, aux_ref, in_ref, out_ref):
    blocks = in_ref.shape[0]
    place = lax.rem(lax.axis_index("ctx") + (blocks - first), blocks)
    owner = lax.div(place * heads, blocks)
    decay = aux_ref[2:3, pl.ds(pl.multiple_of(owner * DH, DH), DH)]
    total = jnp.zeros(in_ref.shape[1:], F32)
    order = range(blocks - 1, -1, -1) if reverse else range(blocks)
    for b in order:
        place = (b - first) % blocks
        out_ref[place] = total
        total = total * decay + in_ref[place]


def inner_kernel(
    rows_ref, gain_ref, q_hbm, k_hbm, v_hbm, out_ref, aux_ref, q_ref, k_ref, v_ref, sems
):
    count, width = k_ref.shape
    aux_ref[...] = rows_ref[...]
    aux_ref[0:1, :] = gain_ref[...]
    wait(fetch(((q_hbm, q_ref), (k_hbm, k_ref), (v_hbm, v_ref)), sems))
    for h in range(width // DH):
        table = band(rows_ref[1:2, head(h)], count)
        for a in range(count // TILE):
            here = slice(a * TILE, (a + 1) * TILE)
            seen = (a + 1) * TILE
            scores = dot(q_ref[here, head(h)], k_ref[:seen, head(h)], NT)
            weights = (scores * table[:, count - seen :]).astype(BF16)
            out_ref[here, head(h)] = dot(weights, v_ref[:seen, head(h)], NN)


def attend_kernel(aux_ref, q_ref, g_ref, inner_ref, prefix_ref, att_ref, sums_ref):
    count, width = q_ref.shape
    squares = jnp.zeros((count, DH), F32)
    crossing = jnp.zeros((count, DH), F32)
    for h in range(width // DH):
        rate = aux_ref[1:2, head(h)]
        weight = rising(rate, count, 1.0)
        attended = (
            inner_ref[:, head(h)] + dot_wide(q_ref[:, head(h)], prefix_ref[head(h), :]) * weight
        )
        att_ref[:, head(h)] = attended
        squares += attended * attended
        crossing += g_ref[:, head(h)].astype(F32) * aux_ref[0:1, head(h)] * attended
    both = jnp.concatenate(to_rows(squares) + to_rows(crossing), axis=0)
    for j in range(sums_ref.shape[0]):
        sums_ref[j] = both


def norm_scales(total, sums_ref):
    tiles = sums_ref.shape[1] // 2
    table = jnp.sum(sums_ref[...], axis=0) / total
    rinv = lax.rsqrt(table[:tiles, :] + 1e-06)
    factor = rinv * rinv * rinv * table[tiles:, :]
    return rinv, factor, tiles


def norm_kernel(
    total, aux_ref, q_ref, g_ref, att_ref, sums_ref, grad_ref, state_ref
):
    count, width = g_ref.shape
    rinv, factor, tiles = norm_scales(total, sums_ref)
    rinv, factor = to_columns(rinv, 0, tiles), to_columns(factor, 0, tiles)
    for h in range(width // DH):
        scaled = g_ref[:, head(h)].astype(F32) * aux_ref[0:1, head(h)]
        grad = (rinv * scaled - att_ref[:, head(h)] * factor).astype(BF16)
        grad_ref[:, head(h)] = grad
        weight = rising(aux_ref[1:2, head(h)], count, 0.0)
        both = jnp.concatenate(halves(grad.astype(F32) * weight), axis=1)
        sums = dot(q_ref[:, head(h)], both, TN)
        state_ref[head(h), :] = sums[:, :DH] + sums[:, DH:]


def query_kernel(
    total, aux_ref, q_hbm, k_hbm, v_hbm, d_ref, prefix_ref, att_ref, sums_ref,
    normed_ref, dq_ref, dk_ref, dv_ref, q_ref, k_ref, v_ref, sems,
):
    count, width = k_ref.shape
    copies = fetch(((q_hbm, q_ref), (k_hbm, k_ref), (v_hbm, v_ref)), sems)
    rinv, _, tiles = norm_scales(total, sums_ref)
    rinv = to_columns(rinv, 0, tiles)
    for h in range(width // DH):
        normed_ref[:, head(h)] = (att_ref[:, head(h)] * rinv * aux_ref[0:1, head(h)]).astype(BF16)
    wait(copies)
    for h in range(width // DH):
        rate = aux_ref[1:2, head(h)]
        table = band(rate, count)
        weight = rising(rate, count, 1.0)
        past = dot_wide(d_ref[:, head(h)], prefix_ref[head(h), :].T) * weight
        for a in range(count // TILE):
            here = slice(a * TILE, (a + 1) * TILE)
            seen = (a + 1) * TILE
            scores = dot(d_ref[here, head(h)], v_ref[:seen, head(h)], NT)
            grads = (scores * table[:, count - seen :]).astype(BF16)
            dq_ref[here, head(h)] = (
                dot(grads, k_ref[:seen, head(h)], NN) + past[here, :]
            ).astype(BF16)
        if h == 0:
            pair_grads(table, q_ref, k_ref, v_ref, d_ref, head(0), dk_ref, dv_ref, head(0))


def pair_grads(table, q_ref, k_ref, v_ref, d_ref, at, dk_ref, dv_ref, to):
    count = q_ref.shape[0]
    for a in range(count // TILE):
        here = slice(a * TILE, (a + 1) * TILE)
        seen = (a + 1) * TILE
        part = table[:, count - seen :]
        q, d = q_ref[here, at], d_ref[here, at]
        weights = (dot(q, k_ref[:seen, at], NT) * part).astype(BF16)
        grads = (dot(d, v_ref[:seen, at], NT) * part).astype(BF16)
        dk, dv = dot(grads, q, TN), dot(weights, d, TN)
        if a:
            before = slice(0, a * TILE)
            dk_ref[before, to] += dk[before, :]
            dv_ref[before, to] += dv[before, :]
        dk_ref[here, to] = dk[here, :]
        dv_ref[here, to] = dv[here, :]


def back_kernel(
    aux_ref, q_hbm, k_hbm, v_hbm, d_hbm, dk_ref, dv_ref, q_ref, k_ref, v_ref, d_ref, sems
):
    count, width = q_ref.shape
    wait(fetch(((q_hbm, q_ref), (k_hbm, k_ref), (v_hbm, v_ref), (d_hbm, d_ref)), sems))
    for h in range(1, width // DH):
        table = band(aux_ref[1:2, head(h)], count)
        pair_grads(table, q_ref, k_ref, v_ref, d_ref, head(h), dk_ref, dv_ref, head(h - 1))


def final_kernel(
    aux_ref, k_ref, v_ref, suffix_ref, dk0_ref, dv0_ref, dk_ref, dv_ref, kout_hbm, vout_hbm, kout_ref, vout_ref, sems
):
    count, width = k_ref.shape
    copies = []
    for h in range(width // DH):
        tail = falling(aux_ref[1:2, head(h)], count, 1.0)
        suffix = suffix_ref[head(h), :]
        kout_ref[:, head(h)] = (
            (dk_ref[:, head(h - 1)] if h else dk0_ref[...]) + dot_wide(v_ref[:, head(h)], suffix.T) * tail
        ).astype(BF16)
        vout_ref[:, head(h)] = (
            (dv_ref[:, head(h - 1)] if h else dv0_ref[...]) + dot_wide(k_ref[:, head(h)], suffix) * tail
        ).astype(BF16)
        for index, (held, out) in enumerate(((kout_ref, kout_hbm), (vout_ref, vout_hbm))):
            copy = pltpu.make_async_copy(
                held.at[:, head(h)], out.at[:, head(h)], sems.at[2 * h + index]
            )
            copy.start()
            copies.append(copy)
    wait(copies)


def call(kernel, shapes, specs, *args, name, flops, size, mib=8, out_specs=None, scratch=()):
    return pl.pallas_call(
        kernel,
        out_shape=shapes,
        in_specs=specs,
        out_specs=out_specs or tuple(VMEM for _ in shapes),
        scratch_shapes=scratch,
        compiler_params=pltpu.CompilerParams(vmem_limit_bytes=mib * 2**20),
        cost_estimate=pl.CostEstimate(flops=flops, bytes_accessed=size, transcendentals=0),
        name=name,
    )(*args)


def exchange(pieces, axis, first):
    size = lax.axis_size(axis)
    order = [(first + j) % size for j in range(size)]
    return lax.all_to_all(pieces, axis, 0, 0, tiled=True, axis_index_groups=[order])


def scan(state, aux, heads, first, reverse):
    pieces = state.reshape(lax.axis_size("ctx"), -1, DH)
    mine = exchange(pieces, "ctx", first)
    (sums,) = call(
        functools.partial(scan_kernel, reverse, first, heads),
        (jax.ShapeDtypeStruct(mine.shape, F32),),
        [VMEM, VMEM],
        aux, mine,
        name="scan", flops=2 * mine.size, size=2 * mine.size * 4, mib=2,
    )
    return exchange(sums, "ctx", first).reshape(state.shape)


def local(queries, keys, values, out_grad, decay_rate, gain):
    count, width = queries.shape
    heads = decay_rate.shape[0]
    shape = jax.ShapeDtypeStruct
    whole, state_shape = (count, width), (width, DH)
    groups = lax.axis_size("head")
    middle, late = FIRST_CTX, FIRST_HEAD
    pair = 2 * count * count * DH * heads
    wide = 4 * count * DH * DH * heads
    unit = count * width
    far_rate, far_q, far_k, far_v = (
        pltpu.with_memory_space_constraint(array, pltpu.HBM)
        for array in (decay_rate, queries, keys, values)
    )
    block = pltpu.VMEM(whole, BF16)
    state, rows = call(
        state_kernel, (shape(state_shape, F32), shape((8, width), F32)), [ANY] * 3, far_rate, far_k, far_v,
        name="state", flops=wide, size=4 * unit,
        scratch=[pltpu.SMEM((heads,), F32), block, block, pltpu.SemaphoreType.DMA((3,))],
    )
    inner, aux = call(
        inner_kernel, (shape(whole, F32), shape((8, width), F32)), [VMEM] * 2 + [ANY] * 3,
        rows, gain[None, :], far_q, far_k, far_v,
        name="inner", flops=2 * pair, size=10 * unit,
        scratch=[block, block, block, pltpu.SemaphoreType.DMA((3,))],
    )
    prefix = scan(state, aux, heads, middle, False)
    attended, sums = call(
        attend_kernel,
        (shape(whole, F32), shape((groups, 2 * count // TILE, TILE), F32)), [VMEM] * 5,
        aux, queries, out_grad, inner, prefix,
        name="attend", flops=wide, size=12 * unit,
    )
    sums = exchange(sums, "head", late)
    total = float(heads * groups * DH)
    grad, state = call(
        functools.partial(norm_kernel, total),
        (shape(whole, BF16), shape(state_shape, F32)), [VMEM] * 5,
        aux, queries, out_grad, attended, sums,
        name="norm", flops=wide, size=12 * unit,
    )
    one, rest = shape((count, DH), F32), shape((count, width - DH), F32)
    normed, dq, dk0, dv0 = call(
        functools.partial(query_kernel, total),
        (shape(whole, BF16), shape(whole, BF16), one, one), [VMEM] + [ANY] * 3 + [VMEM] * 4,
        aux, far_q, far_k, far_v, grad, prefix, attended, sums,
        name="query", flops=2 * pair, size=16 * unit,
        scratch=[block, block, block, pltpu.SemaphoreType.DMA((3,))],
    )
    aux, normed, dq = lax.optimization_barrier((aux, normed, dq))
    suffix = scan(state, aux, heads, middle, True)
    dk, dv = call(
        back_kernel, (rest, rest), [VMEM] + [ANY] * 4,
        aux, far_q, far_k, far_v, pltpu.with_memory_space_constraint(grad, pltpu.HBM),
        name="back", flops=4 * pair, size=16 * unit,
        scratch=[block, block, block, block, pltpu.SemaphoreType.DMA((4,))],
    )
    dk, dv = call(
        final_kernel, (shape(whole, BF16), shape(whole, BF16)), [VMEM] * 8,
        aux, keys, values, suffix, dk0, dv0, dk, dv,
        name="final", flops=2 * wide, size=20 * unit, out_specs=(ANY, ANY),
        scratch=[block, block, pltpu.SemaphoreType.DMA((2 * heads,))],
    )
    return normed, dq, dk, dv


def solution(mesh):
    tokens = P("ctx", "head")
    return jax.shard_map(
        local,
        mesh=mesh,
        in_specs=(tokens,) * 4 + (P("head"),) * 2,
        out_specs=(tokens,) * 4,
        check_vma=False,
    )
```
